256 devices in a mesh: expert: 32 (over z, y_hi, core), hid: 8 (over y_lo, x).
Axes of the slice: x: 4, y: 4 (y_hi: 2, y_lo: 2; y = y_hi * 2 + y_lo), z: 8, core: 2. Of those that a mesh axis runs over, the one named last changes fastest.
Arguments:
- tokens: bfloat16 [4096, 7168], P('expert', 'hid'), may hold values from -6 to 6
- cotangent: bfloat16 [4096, 7168], P('expert', 'hid'), may hold values from -6 to 6
- expert_ids: int32 [4096, 8], P('expert'), may hold values from 0 to 31, all different within a row; in each aligned block of 128 rows (0 to 127, 128 to 255, ...) at most 40 rows name the same one
- gate_weights: float32 [4096, 8], P('expert'), may hold values from 0.1 to 0.6
- owner_old: int32 [32], replicated, may hold values from 0 to 31, as said below
- owner_new: int32 [32], replicated, may hold values from 0 to 31, as said below
- w_gate: bfloat16 [32, 1024, 7168], P('expert', None, 'hid'), may hold values from -0.0625 to 0.0625
- w_down: bfloat16 [32, 1024, 7168], P('expert', None, 'hid'), may hold values from -0.1875 to 0.1875
Outputs:
- layer_out: bfloat16 [4096, 7168], P('expert', 'hid')
- token_grads: bfloat16 [4096, 7168], P('expert', 'hid')
- grad_gate: bfloat16 [32, 1024, 7168], P('expert', None, 'hid')
- grad_down: bfloat16 [32, 1024, 7168], P('expert', None, 'hid')
The draws below stay inside these ranges and needn't reach their ends.
Inputs may be any that keep to these rules, and one draw needn't show every extreme that they name: `expert_ids`: each row names 8 different experts. Within the rows of one device (aligned blocks of 128 rows) no expert is named more than 40 times, and in some block an expert is named exactly 40 times. `owner_old`: A permutation of the experts over the device indices. `owner_new`: A permutation that agrees with owner_old on all experts but exactly 8 of them.
All inputs are finite; a program needn't handle non-finite values.
Results may differ from the reference program's by a relative error of at most 0.025.
Values may be sent and summed in bfloat16 or wider, within the bound.
A program may use at most 128 MiB of HBM per device.

```python
import math
import jax
import jax.numpy as jnp
import numpy as np
from jax import lax

D = 7168
FF = 1024
TOP = 8
TOK_DEV = 128
EXPERTS = 32
TOKENS = 4096
CAP = 40
MOVING = 8
SLICES = 8


def table_pair(key):
    old_table = jax.random.permutation(jax.random.fold_in(key, 11), EXPERTS).astype(jnp.int32)
    shuffled = jax.random.permutation(jax.random.fold_in(key, 12), EXPERTS)
    moving = shuffled[:MOVING]
    new_table = old_table.at[moving].set(old_table[jnp.roll(moving, -1)])
    return (old_table, new_table)


def draw_owner_old(key, part):
    tables = table_pair(key)
    return tables[0]


def draw_owner_new(key, part):
    tables = table_pair(key)
    return tables[1]


def steps_of(stream_key, dims, cuts, smallest, high):
    def one(axis_at, parts):
        steps = jax.random.uniform(jax.random.fold_in(jax.random.fold_in(stream_key, 6), axis_at), (parts,), jnp.float32, smallest / len(cuts), high / len(cuts))
        return jnp.repeat(jnp.exp(steps), dims[axis_at] // parts).reshape((-1,) + (1,) * (len(dims) - axis_at - 1))

    gain = one(*cuts[0])
    for cut in cuts[1:]:
        gain = gain * one(*cut)
    return gain


def assign_block(own_key, own, number, rows, count, top, reach, slope):
    order = jax.random.permutation(own_key, count)
    heavy_load, common = shares(count, rows * top, reach, slope, True), shares(count, rows * top, reach, slope, False)
    places = jnp.arange(count)

    def named(tallies, rotation):
        used = int((tallies > 0).sum())
        fixed = max(1, used // 4)
        passed = fixed + (places - fixed + rotation * (used - fixed)) % max(1, count - fixed)
        return jnp.zeros((count,), jnp.int32).at[order[jnp.where(places < fixed, places, passed)]].set(jnp.asarray(tallies, jnp.int32))

    tallies = jnp.where(number % 4 == 0, named(heavy_load, number // 4), named(common, number - number // 4 - 1))
    mixed = jax.random.permutation(jax.random.fold_in(own, 3), count)
    giver, receiver = mixed[0:count // 2 * 2:2], mixed[1:count // 2 * 2:2]
    slack = jnp.minimum(tallies[giver] - 1, reach - tallies[receiver]) // 2
    slack = jnp.where((giver == order[0]) | (receiver == order[0]) | (tallies[receiver] == 0), 0, jnp.maximum(slack, 0))
    passed = jax.random.randint(jax.random.fold_in(own, 4), (count // 2,), 0, 1 << 20) % (slack + 1)
    tallies = tallies.at[giver].add(-passed).at[receiver].add(passed)
    items = jnp.searchsorted(jnp.cumsum(tallies), jnp.arange(rows * top), side="right").astype(jnp.int32)
    grid = items.reshape(top, rows).T
    grid = grid[jax.random.permutation(jax.random.fold_in(own, 1), rows)]
    rotation = jax.random.randint(jax.random.fold_in(own, 2), (rows, 1), 0, top)
    return jnp.take_along_axis(grid, (jnp.arange(top)[None, :] + rotation) % top, axis=1)


def shares(amount, total, reach, skew, full):
    loads = [(1 << 20) // math.isqrt(rank ** skew) + 1 for rank in range(1, amount + 1)]
    largest = reach if full else min(reach, max(-(-total // amount), total * loads[0] // sum(loads)))
    least = 1 if total - largest >= amount - 1 else 0
    counts, rest = [largest] + [least] * (amount - 1), total - largest - least * (amount - 1)
    while rest > 0:
        candidates = [i for i in range(1, amount) if counts[i] < largest] or [i for i in range(1, amount) if counts[i] < reach]
        pool, remaining = sum([loads[i] for i in candidates]), rest
        for i in candidates:
            addition = min(reach - counts[i], max(1, remaining * loads[i] // pool), rest)
            counts[i] = counts[i] + addition
            rest = rest - addition
    return np.array(counts)


def scatter_about(stream_key, extent, width, limit, split=(), kind=jnp.bfloat16):
    result = jax.random.normal(stream_key, extent, jnp.float32) * width
    if len(split) > 0:
        result = steps_of(stream_key, extent, split, -0.22, 0.18) * result
    return jnp.clip(result, min=-limit, max=limit).astype(kind)


def setup_inputs(seed: int = 0) -> dict:
    splits = jax.random.split(jax.random.key(seed), 9)
    tokens = scatter_about(splits[0], (TOKENS, D), 1.0, 6.0, ((0, 32), (1, 8)))
    cotangent = scatter_about(splits[1], (TOKENS, D), 1.0, 6.0, ((0, 32), (1, 8)))
    expert_ids_keys = jax.random.split(jax.random.fold_in(splits[2], 1), TOKENS // TOK_DEV)
    expert_ids_turns = jax.random.permutation(jax.random.fold_in(splits[2], 3), TOKENS // TOK_DEV)
    expert_ids = jax.vmap(lambda own, number: assign_block(jax.random.fold_in(splits[2], 2), own, number, TOK_DEV, EXPERTS, TOP, CAP, 2))(expert_ids_keys, expert_ids_turns).reshape((TOKENS, TOP))
    gate_weights = jnp.clip(0.1 + 0.5 * jax.random.uniform(splits[3], (TOKENS, TOP), jnp.float32) ** steps_of(splits[3], (TOKENS, TOP), ((0, 32),), -0.2, 0.2), 0.1, 0.6)
    owner_old = draw_owner_old(jax.random.fold_in(splits[8], 71), 0)
    owner_new = draw_owner_new(jax.random.fold_in(splits[8], 71), 0)
    w_gate = scatter_about(splits[6], (EXPERTS, FF, D), D ** -0.5, 0.0625, ((0, 32), (2, 8)))
    w_down = scatter_about(splits[7], (EXPERTS, FF, D), FF ** -0.5, 0.1875, ((0, 32), (2, 8)))
    return {"tokens": tokens, "cotangent": cotangent, "expert_ids": expert_ids, "gate_weights": gate_weights, "owner_old": owner_old, "owner_new": owner_new, "w_gate": w_gate, "w_down": w_down}


def slots_of(expert_ids):
    blocks = expert_ids.reshape(EXPERTS, TOK_DEV, TOP)
    labels = jnp.arange(EXPERTS, dtype=jnp.int32)
    onehot = (blocks[..., None] == labels).astype(jnp.int32)
    per_token = jnp.sum(onehot, axis=2, dtype=jnp.int32)
    before = jnp.cumsum(per_token, axis=1, dtype=jnp.int32) - per_token
    return jnp.sum(onehot * before[:, :, None, :], axis=3, dtype=jnp.int32)


def split_product(left_mat, right_mat):
    row_count = left_mat.shape[0]
    left_parts = left_mat.reshape(row_count, SLICES, D // SLICES).astype(jnp.float32)
    right_parts = right_mat.reshape(FF, SLICES, D // SLICES).astype(jnp.float32)
    part_terms = jnp.einsum('rjd,fjd->jrf', left_parts, right_parts)
    part_terms = lax.optimization_barrier(part_terms.astype(jnp.bfloat16))
    return jnp.sum(part_terms.astype(jnp.float32), axis=0)


def expert_pass(rows_mat, cot_mat, gate_mat, down_mat):
    pre_act = split_product(rows_mat, gate_mat)
    back_act = split_product(cot_mat, down_mat)
    sigmoid_pre = jax.nn.sigmoid(pre_act)
    hidden = (pre_act * sigmoid_pre).astype(jnp.bfloat16)
    slope_rows = (back_act * sigmoid_pre * (1.0 + pre_act * (1.0 - sigmoid_pre))).astype(jnp.bfloat16)
    expert_out = jnp.dot(hidden, down_mat, preferred_element_type=jnp.float32).astype(jnp.bfloat16)
    back_rows = jnp.dot(slope_rows, gate_mat, preferred_element_type=jnp.float32).astype(jnp.bfloat16)
    gate_step = jnp.dot(slope_rows.T, rows_mat, preferred_element_type=jnp.float32).astype(jnp.bfloat16)
    down_step = jnp.dot(hidden.T, cot_mat, preferred_element_type=jnp.float32).astype(jnp.bfloat16)
    return expert_out, back_rows, gate_step, down_step


def reference(tokens, cotangent, expert_ids, gate_weights, owner_old, owner_new, w_gate, w_down):
    slot_rank = slots_of(expert_ids)
    block_ids = jnp.arange(EXPERTS, dtype=jnp.int32)[:, None, None]
    target = owner_old[expert_ids].reshape(EXPERTS, TOK_DEV, TOP).astype(jnp.int32)
    position = target * (EXPERTS * CAP) + block_ids * CAP + slot_rank
    pair_ids = jnp.arange(TOKENS * TOP, dtype=jnp.int32)
    filler = jnp.full((EXPERTS * EXPERTS * CAP,), TOKENS * TOP, dtype=jnp.int32)
    filler = filler.at[position.reshape(-1)].set(pair_ids).reshape(EXPERTS, EXPERTS * CAP)
    padded_tokens = jnp.concatenate([tokens, jnp.zeros((1, D), jnp.bfloat16)], axis=0)
    padded_cot = jnp.concatenate([cotangent, jnp.zeros((1, D), jnp.bfloat16)], axis=0)
    padded_gates = jnp.concatenate([gate_weights.reshape(-1), jnp.zeros((1,), jnp.float32)], axis=0)

    def per_expert(expert_index):
        chosen = filler[expert_index]
        source = chosen // TOP
        rows_mat = padded_tokens[source]
        cot_mat = (padded_cot[source].astype(jnp.float32) * padded_gates[chosen][:, None]).astype(jnp.bfloat16)
        return expert_pass(rows_mat, cot_mat, w_gate[expert_index], w_down[expert_index])

    expert_out, back_rows, gate_step, down_step = lax.map(per_expert, jnp.arange(EXPERTS, dtype=jnp.int32))
    flat_out = expert_out.reshape(-1, D)
    flat_back = back_rows.reshape(-1, D)
    gate_blocks = gate_weights.reshape(EXPERTS, TOK_DEV, TOP)

    def combine(inputs):
        where_rows, weight_rows = inputs
        picked = flat_out[where_rows].astype(jnp.float32)
        layer_part = jnp.sum(picked * weight_rows[:, :, None], axis=1).astype(jnp.bfloat16)
        grads_part = jnp.sum(flat_back[where_rows].astype(jnp.float32), axis=1).astype(jnp.bfloat16)
        return layer_part, grads_part

    layer_out, token_grads = lax.map(combine, (position, gate_blocks))
    source_of = jnp.zeros((EXPERTS,), jnp.int32).at[owner_new].set(owner_old)
    grad_gate = gate_step[source_of]
    grad_down = down_step[source_of]
    return layer_out.reshape(TOKENS, D), token_grads.reshape(TOKENS, D), grad_gate, grad_down
```

```python
import functools

import jax
import jax.numpy as jnp
from jax import lax
from jax.experimental import pallas as pl
from jax.experimental.pallas import tpu as pltpu
from jax.sharding import PartitionSpec as P

MESH = pl.DeviceIdType.MESH
BF = jnp.bfloat16
F32 = jnp.float32
VMEM_LIMIT = 62 << 20
NZ, CAP, TOK, HALF, QUART = 8, 40, 128, 64, 32
ROWS, PAIR = 1280, 80


def place():
    e, d = lax.axis_index("expert"), lax.axis_index("hid")
    return e // 4, (e // 2) % 2, e % 2, d // 4, d % 4


class Links:
    def __init__(self, send_sem, recv_sem):
        self.z, self.h, self.c, self.lo, self.x = place()
        self.send_sem, self.recv_sem, self.used, self.sent = send_sem, recv_sem, 0, []

    def at(self, z=None, h=None, c=None, lo=None, x=None):
        z = self.z if z is None else z
        h = self.h if h is None else h
        c = self.c if c is None else c
        lo = self.lo if lo is None else lo
        x = self.x if x is None else x
        return (z * 4 + h * 2 + c, lo * 4 + x)

    def dz(self, k):
        return (self.z + k + NZ) % NZ

    def dx(self, k):
        return (self.x + k + 4) % 4

    def barrier(self):
        peers = [
            self.at(z=self.dz(1)),
            self.at(z=self.dz(-1)),
            self.at(h=1 - self.h),
            self.at(c=1 - self.c),
            self.at(x=self.dx(1)),
            self.at(x=self.dx(-1)),
            self.at(lo=1 - self.lo),
        ]
        sem = pltpu.get_barrier_semaphore()
        for peer in peers:
            pl.semaphore_signal(sem, inc=1, device_id=peer, device_id_type=MESH)
        pl.semaphore_wait(sem, len(peers))

    def new(self):
        self.used += 1
        return self.used - 1

    def send(self, src, dst, peer, sem=None):
        i = self.new()
        copy = pltpu.make_async_remote_copy(
            src_ref=src,
            dst_ref=dst,
            send_sem=self.send_sem.at[i],
            recv_sem=self.recv_sem.at[i if sem is None else sem],
            device_id=peer,
            device_id_type=MESH,
        )
        copy.start()
        self.sent.append(copy)
        return i

    def arrive(self, ref, i):
        pltpu.make_async_copy(ref, ref, self.recv_sem.at[i]).wait()

    def drain(self):
        for copy in self.sent:
            copy.wait_send()
        self.sent = []


def gather_flow(net, own, full, local_sem):
    z, h, c = net.z, net.h, net.c
    other_y, other_c = net.at(h=1 - h), net.at(c=1 - c)
    right, left = net.at(z=net.dz(1)), net.at(z=net.dz(-1))
    me = c * NZ + z
    ra, rb = pl.ds(0, HALF), pl.ds(HALF, HALF)
    a_first, a_last = pl.ds(0, QUART), pl.ds(QUART, QUART)
    b_first, b_last = pl.ds(HALF, QUART), pl.ds(HALF + QUART, QUART)
    core_sems = [net.new() for _ in range(NZ)]
    keep = pltpu.make_async_copy(own, full.at[me, h], local_sem)
    keep.start()
    ya = net.send(own.at[ra], full.at[me, h, ra], other_y)
    b_right = net.send(own.at[rb], full.at[me, h, rb], right)
    b_left = net.send(own.at[rb], full.at[me, h, rb], left)
    keep.wait()
    yb = [net.send(full.at[me, h, rb], full.at[me, h, rb], other_y)]

    def to_core(k, what):
        slot = c * NZ + net.dz(k)
        net.send(full.at[(slot,) + what], full.at[(slot,) + what], other_c, sem=core_sems[k % NZ])

    to_core(0, (h, slice(None)))
    both = slice(None)
    net.arrive(full.at[me, 1 - h, ra], ya)
    a_right = net.send(full.at[me, both, ra], full.at[me, both, ra], right)
    a_left = net.send(full.at[me, both, ra], full.at[me, both, ra], left)
    to_core(0, (1 - h, ra))
    yield
    pending = [(0, yb[0])]
    for k in range(4):
        zr, zl = c * NZ + net.dz(-1 - k), c * NZ + net.dz(1 + k)
        last, nxt_last = k == 3, k == 2
        br, bl = (b_first, b_last) if last else (rb, rb)
        net.arrive(full.at[zr, h, br], b_right)
        if not last:
            rows = b_first if nxt_last else rb
            b_right = net.send(full.at[zr, h, rows], full.at[zr, h, rows], right)
        net.arrive(full.at[zl, h, bl], b_left)
        if not last:
            rows = b_last if nxt_last else rb
            b_left = net.send(full.at[zl, h, rows], full.at[zl, h, rows], left)
        fresh = [(-1 - k, net.send(full.at[zr, h, rb], full.at[zr, h, rb], other_y))]
        to_core(-1 - k, (h, rb))
        if not last:
            fresh.append((1 + k, net.send(full.at[zl, h, rb], full.at[zl, h, rb], other_y)))
            to_core(1 + k, (h, rb))
        ar, al = (a_first, a_last) if last else (ra, ra)
        net.arrive(full.at[zr, both, ar], a_right)
        if not last:
            rows = a_first if nxt_last else ra
            a_right = net.send(full.at[zr, both, rows], full.at[zr, both, rows], right)
        net.arrive(full.at[zl, both, al], a_left)
        if not last:
            rows = a_last if nxt_last else ra
            a_left = net.send(full.at[zl, both, rows], full.at[zl, both, rows], left)
        to_core(-1 - k, (both, ra))
        if not last:
            to_core(1 + k, (both, ra))
        for d, sem in pending:
            slot = c * NZ + net.dz(d)
            net.arrive(full.at[slot, 1 - h, rb], sem)
            to_core(d, (1 - h, rb))
        pending = fresh
        yield
    for d, sem in pending:
        slot = c * NZ + net.dz(d)
        net.arrive(full.at[slot, 1 - h, rb], sem)
        to_core(d, (1 - h, rb))
    for k in range(NZ):
        net.arrive(full.at[(1 - c) * NZ + net.dz(k)], core_sems[k])
    yield


def small_gather(net, own, full, local_sem):
    z, h, c = net.z, net.h, net.c
    right, left = net.at(z=net.dz(1)), net.at(z=net.dz(-1))
    me = c * NZ + z
    keep = pltpu.make_async_copy(own, full.at[h, me], local_sem)
    keep.start()
    y = net.send(own, full.at[h, me], net.at(h=1 - h))
    keep.wait()
    net.arrive(full.at[1 - h, me], y)
    r = net.send(full.at[:, me], full.at[:, me], right)
    l = net.send(full.at[:, me], full.at[:, me], left)
    yield
    for k in range(4):
        zr, zl = c * NZ + net.dz(-1 - k), c * NZ + net.dz(1 + k)
        net.arrive(full.at[:, zr], r)
        if k < 3:
            r = net.send(full.at[:, zr], full.at[:, zr], right)
            net.arrive(full.at[:, zl], l)
            if k < 2:
                l = net.send(full.at[:, zl], full.at[:, zl], left)
        yield
    mine, theirs = pl.ds(pl.multiple_of(c * NZ, NZ), NZ), pl.ds(pl.multiple_of((1 - c) * NZ, NZ), NZ)
    i = net.send(full.at[:, mine], full.at[:, mine], net.at(c=1 - c))
    net.arrive(full.at[:, theirs], i)
    yield


def cols(xt, lo=None):
    if lo is None:
        return pl.ds(pl.multiple_of(xt * 256, 256), 256)
    return pl.ds(pl.multiple_of(xt * 256 + lo * 128, 128), 128)


def reduce_flow(net, part, out, hop_r, hop_l, in_r, in_l, y_out, y_in):
    x, lo = net.x, net.lo
    right, left = net.at(x=net.dx(1)), net.at(x=net.dx(-1))
    n = ROWS // 2
    r0, r1 = pl.ds(0, n), pl.ds(n, n)
    far, nr, nl, own = cols(net.dx(2)), cols(net.dx(1)), cols(net.dx(-1)), cols(x)
    s1 = net.send(part.at[r0, far], hop_r, right)
    s2 = net.send(part.at[r1, far], hop_l, left)
    yield
    s3 = net.send(part.at[r1, nr], in_r.at[r1], right)
    s4 = net.send(part.at[r0, nl], in_l.at[r0], left)
    yield
    tile = 160

    def add(dst_rows, where, src):
        def body(i, carry):
            at = pl.multiple_of(i * tile, tile)
            rows = pl.ds(pl.multiple_of(dst_rows + at, tile), tile)
            part[rows, where] = (
                part[rows, where].astype(F32) + src[pl.ds(at, tile), :].astype(F32)
            ).astype(BF)
            return carry

        lax.fori_loop(0, n // tile, body, 0)

    net.arrive(hop_r, s1)
    add(0, nr, hop_r)
    s5 = net.send(part.at[r0, nr], in_r.at[r0], right)
    net.arrive(hop_l, s2)
    add(n, nl, hop_l)
    s6 = net.send(part.at[r1, nl], in_l.at[r1], left)
    yield
    waits = {0: ((in_r, s5), (in_l, s4)), 1: ((in_r, s3), (in_l, s6))}
    ys = []
    for half in (1, 0):
        rows_half = (r0, r1)[half]
        for buf, sem in waits[half]:
            net.arrive(buf.at[rows_half], sem)

        def total(i, carry):
            rows = pl.ds(pl.multiple_of(half * n + i * tile, tile), tile)
            for side, keep in ((lo, True), (1 - lo, False)):
                inner = pl.ds(pl.multiple_of(side * 128, 128), 128)
                acc = (
                    part[rows, cols(x, side)].astype(F32)
                    + in_r[rows, inner].astype(F32)
                    + in_l[rows, inner].astype(F32)
                )
                if keep:
                    out[rows, :] = acc
                else:
                    y_out[rows, :] = acc.astype(BF)
            return carry

        lax.fori_loop(0, n // tile, total, 0)
        ys.append((half, net.send(y_out.at[rows_half], y_in.at[rows_half], net.at(lo=1 - lo))))
        yield
    for half, sem in ys:
        net.arrive(y_in.at[(r0, r1)[half]], sem)

        def last(i, carry):
            rows = pl.ds(pl.multiple_of(half * n + i * tile, tile), tile)
            out[rows, :] = out[rows, :] + y_in[rows, :].astype(F32)
            return carry

        lax.fori_loop(0, n // tile, last, 0)
    yield


def run_together(*flows):
    flows = list(flows)
    while flows:
        for flow in list(flows):
            try:
                next(flow)
            except StopIteration:
                flows.remove(flow)


def ranks(info, expert, tri, rank_ref, weight_ref):
    for side in range(2):
        hit = info[side, :, 0:8, :] == expert[...][0:1, :][None]
        mask = jnp.max(jnp.where(hit, 1.0, 0.0), axis=1)
        weight = jnp.sum(jnp.where(hit, info[side, :, 8:16, :], 0.0), axis=1)
        before = jnp.dot(mask.astype(BF), tri[...], preferred_element_type=F32)
        where = pl.ds(side * TOK, TOK)
        rank_ref[:, where] = jnp.where(mask > 0.5, before + float(side * CAP), -1.0)
        weight_ref[:, where] = weight


def picker(rank_ref, p):
    slots = lax.broadcasted_iota(jnp.int32, (PAIR, 2 * TOK), 0).astype(F32)
    return jnp.where(slots == rank_ref[pl.ds(p, 1), :], 1.0, 0.0)


def dispatch_kernel(
    tok, cot, info, wg, wd, eold, enew, tri,
    hid_o, slope_o, rows_new, cot_new,
    tok_all, cot_all, info_all, rows, part_a, part_b, acc_a, acc_b,
    hop_r, hop_l, in_r, in_l, y_out, y_in,
    rank_old, weight_old, rank_new, weight_new,
    local_sem, send_sem, recv_sem,
):
    net = Links(send_sem, recv_sem)
    net.barrier()
    small = small_gather(net, info, info_all, local_sem.at[0])
    toks = gather_flow(net, tok, tok_all, local_sem.at[1])
    cots = gather_flow(net, cot, cot_all, local_sem.at[2])
    run_together(small, toks)
    next(cots)
    ranks(info_all, eold, tri, rank_old, weight_old)
    ranks(info_all, enew, tri, rank_new, weight_new)
    next(cots)

    def pick_tok(p, carry):
        block = tok_all[p].reshape(2 * TOK, tok_all.shape[-1])
        at = pl.ds(pl.multiple_of(p * PAIR, 16), PAIR)
        for rank_ref, out in ((rank_old, rows), (rank_new, rows_new)):
            sel = picker(rank_ref, p).astype(BF)
            out[at, :] = jnp.dot(sel, block, preferred_element_type=F32).astype(BF)
        return carry

    def pick_cot(p, carry):
        block = cot_all[p].reshape(2 * TOK, cot_all.shape[-1])
        at = pl.ds(pl.multiple_of(p * PAIR, 16), PAIR)
        for rank_ref, weight_ref, out in ((rank_old, weight_old, rows), (rank_new, weight_new, cot_new)):
            hit = picker(rank_ref, p)
            weight = jnp.sum(hit * weight_ref[pl.ds(p, 1), :], axis=1, keepdims=True)
            sel = jnp.dot(hit.astype(BF), block, preferred_element_type=F32)
            out[at, :] = (sel * weight).astype(BF)
        return carry

    def project(w, part, shift):
        where = cols(net.dx(shift))
        tile = 320

        def body(i, carry):
            at = pl.ds(pl.multiple_of(i * tile, tile), tile)
            part[at, where] = lax.dot_general(
                rows[at, :], w[where, :], (((1,), (1,)), ((), ())), preferred_element_type=F32
            ).astype(BF)
            return carry

        lax.fori_loop(0, ROWS // tile, body, 0)

    def flow(w, part, out, bufs):
        project(w, part, 2)
        red = reduce_flow(net, part, out, *bufs)
        next(red)
        project(w, part, 1)
        project(w, part, -1)
        next(red)
        project(w, part, 0)
        yield
        yield from red

    bufs_a = [r.at[0] for r in (hop_r, hop_l, in_r, in_l, y_out, y_in)]
    bufs_b = [r.at[1] for r in (hop_r, hop_l, in_r, in_l, y_out, y_in)]
    lax.fori_loop(0, 16, pick_tok, 0)
    next(cots)
    run_together(flow(wg, part_a, acc_a, bufs_a), cots)
    lax.fori_loop(0, 16, pick_cot, 0)
    run_together(flow(wd, part_b, acc_b, bufs_b))

    def act(i, carry):
        at = pl.ds(pl.multiple_of(i * 160, 160), 160)
        pre, back = acc_a[at, :], acc_b[at, :]
        sig = jax.nn.sigmoid(pre)
        hid_o[at, :] = (pre * sig).astype(BF)
        slope_o[at, :] = (back * sig * (1.0 + pre * (1.0 - sig))).astype(BF)
        return carry

    lax.fori_loop(0, ROWS // 160, act, 0)
    net.drain()


def dispatch(tokens, cotangent, info, w_gate, w_down, eold, enew, tri):
    width = tokens.shape[1]
    vm = pl.BlockSpec(memory_space=pltpu.VMEM)
    sds = jax.ShapeDtypeStruct
    half = ROWS // 2
    return pl.pallas_call(
        dispatch_kernel,
        out_shape=(
            sds((ROWS, 128), BF),
            sds((ROWS, 128), BF),
            sds((ROWS, width), BF),
            sds((ROWS, width), BF),
        ),
        in_specs=[vm] * 8,
        out_specs=(vm,) * 4,
        scratch_shapes=[
            pltpu.VMEM((16, 2, TOK, width), BF),
            pltpu.VMEM((16, 2, TOK, width), BF),
            pltpu.VMEM((2, 16, 16, 128), F32),
            pltpu.VMEM((ROWS, width), BF),
            pltpu.VMEM((ROWS, 1024), BF),
            pltpu.VMEM((ROWS, 1024), BF),
            pltpu.VMEM((ROWS, 128), F32),
            pltpu.VMEM((ROWS, 128), F32),
            pltpu.VMEM((2, half, 256), BF),
            pltpu.VMEM((2, half, 256), BF),
            pltpu.VMEM((2, ROWS, 256), BF),
            pltpu.VMEM((2, ROWS, 256), BF),
            pltpu.VMEM((2, ROWS, 128), BF),
            pltpu.VMEM((2, ROWS, 128), BF),
            pltpu.VMEM((16, 256), F32),
            pltpu.VMEM((16, 256), F32),
            pltpu.VMEM((16, 256), F32),
            pltpu.VMEM((16, 256), F32),
            pltpu.SemaphoreType.DMA((3,)),
            pltpu.SemaphoreType.DMA((192,)),
            pltpu.SemaphoreType.DMA((192,)),
        ],
        compiler_params=pltpu.CompilerParams(
            collective_id=0, has_side_effects=True, vmem_limit_bytes=VMEM_LIMIT
        ),
    )(tokens, cotangent, info, w_gate, w_down, eold, enew, tri)


def contract_rows(left_mat, right_mat):
    return lax.dot_general(
        left_mat, right_mat, (((0,), (0,)), ((), ())), preferred_element_type=jnp.float32
    )


def exchange(a):
    return lax.all_to_all(a, "expert", split_axis=0, concat_axis=0, tiled=True)


def per_device(tokens, cotangent, expert_ids, gate_weights, owner_old, owner_new, w_gate, w_down):
    me = lax.axis_index("expert")
    labels = jnp.arange(32, dtype=jnp.int32)
    width = tokens.shape[1]
    info = jnp.concatenate([expert_ids.T.astype(F32), gate_weights.T], axis=0)
    eold = jnp.broadcast_to(jnp.sum(jnp.where(owner_old == me, labels, 0)).astype(F32), (8, 128))
    enew = jnp.broadcast_to(jnp.sum(jnp.where(owner_new == me, labels, 0)).astype(F32), (8, 128))
    lane = jnp.arange(128)
    tri = (lane[:, None] < lane[None, :]).astype(BF)
    gate_here, down_here = w_gate[0], w_down[0]
    hid_s, slope_s, rows_new, cot_new = dispatch(
        tokens, cotangent, info, gate_here, down_here, eold, enew, tri
    )

    def whole(shard):
        g = lax.all_gather(shard, "hid").reshape(2, 4, ROWS, 128)
        return g.transpose(2, 1, 0, 3).reshape(ROWS, 1024)

    moved_to = (owner_new[:, None] == labels[None, :]).astype(jnp.int32)
    source_of = jnp.sum(moved_to * owner_old[:, None], axis=0, dtype=jnp.int32)
    both = jnp.concatenate([hid_s, slope_s], axis=1).reshape(32, CAP, 256)
    moved = exchange(jnp.take(exchange(both), source_of, axis=0)).reshape(ROWS, 256)
    hidden, slope = whole(hid_s), whole(slope_s)
    hidden_new, slope_new = whole(moved[:, :128]), whole(moved[:, 128:])
    expert_out = jnp.dot(hidden, down_here, preferred_element_type=F32).astype(BF)
    back_rows = jnp.dot(slope, gate_here, preferred_element_type=F32).astype(BF)
    grad_gate = contract_rows(slope_new, rows_new).astype(BF)
    grad_down = contract_rows(hidden_new, cot_new).astype(BF)

    onehot = (expert_ids[:, :, None] == labels).astype(jnp.int32)
    per_token = jnp.sum(onehot, axis=1, dtype=jnp.int32)
    before = jnp.cumsum(per_token, axis=0, dtype=jnp.int32) - per_token
    slot_rank = jnp.sum(onehot * before[:, None, :], axis=2, dtype=jnp.int32)
    target = jnp.sum(onehot * owner_old, axis=2, dtype=jnp.int32)
    position = target * CAP + slot_rank

    def back(a):
        a = a.reshape(2, 8, 2, CAP, width).transpose(1, 2, 0, 3, 4).reshape(32, CAP, width)
        return exchange(a).reshape(ROWS, width)

    out_flat, grads_flat = back(expert_out), back(back_rows)
    picked_out = out_flat[position].astype(F32)
    layer_out = jnp.sum(picked_out * gate_weights[:, :, None], axis=1).astype(BF)
    token_grads = jnp.sum(grads_flat[position].astype(F32), axis=1).astype(BF)
    return (layer_out, token_grads, grad_gate[None], grad_down[None])


def solution(mesh):
    return jax.shard_map(
        per_device,
        mesh=mesh,
        in_specs=(
            P("expert", "hid"),
            P("expert", "hid"),
            P("expert", None),
            P("expert", None),
            P(),
            P(),
            P("expert", None, "hid"),
            P("expert", None, "hid"),
        ),
        out_specs=(
            P("expert", "hid"),
            P("expert", "hid"),
            P("expert", None, "hid"),
            P("expert", None, "hid"),
        ),
        check_vma=False,
    )
```

```python
import functools

import jax
import jax.numpy as jnp
from jax import lax
from jax.experimental import pallas as pl
from jax.experimental.pallas import tpu as pltpu
from jax.sharding import PartitionSpec as P

MESH = pl.DeviceIdType.MESH
BF = jnp.bfloat16
F32 = jnp.float32
VMEM_LIMIT = 62 << 20
NZ, CAP, TOK, HALF, QUART = 8, 40, 128, 64, 32
ROWS, PAIR = 1280, 80


def place():
    e, d = lax.axis_index("expert"), lax.axis_index("hid")
    return e // 4, (e // 2) % 2, e % 2, d // 4, d % 4


class Links:
    def __init__(self, send_sem, recv_sem):
        self.z, self.h, self.c, self.lo, self.x = place()
        self.send_sem, self.recv_sem, self.used, self.sent = send_sem, recv_sem, 0, []

    def at(self, z=None, h=None, c=None, lo=None, x=None):
        z = self.z if z is None else z
        h = self.h if h is None else h
        c = self.c if c is None else c
        lo = self.lo if lo is None else lo
        x = self.x if x is None else x
        return (z * 4 + h * 2 + c, lo * 4 + x)

    def dz(self, k):
        return (self.z + k + NZ) % NZ

    def dx(self, k):
        return (self.x + k + 4) % 4

    def barrier(self, all_z=False):
        peers = [self.at(z=self.dz(k)) for k in (range(1, NZ) if all_z else (1, -1))]
        peers += [
            self.at(h=1 - self.h),
            self.at(c=1 - self.c),
            self.at(x=self.dx(1)),
            self.at(x=self.dx(-1)),
            self.at(lo=1 - self.lo),
        ]
        sem = pltpu.get_barrier_semaphore()
        for peer in peers:
            pl.semaphore_signal(sem, inc=1, device_id=peer, device_id_type=MESH)
        pl.semaphore_wait(sem, len(peers))

    def new(self):
        self.used += 1
        return self.used - 1

    def send(self, src, dst, peer, sem=None):
        i = self.new()
        copy = pltpu.make_async_remote_copy(
            src_ref=src,
            dst_ref=dst,
            send_sem=self.send_sem.at[i],
            recv_sem=self.recv_sem.at[i if sem is None else sem],
            device_id=peer,
            device_id_type=MESH,
        )
        copy.start()
        self.sent.append(copy)
        return i

    def arrive(self, ref, i):
        pltpu.make_async_copy(ref, ref, self.recv_sem.at[i]).wait()

    def drain(self):
        for copy in self.sent:
            copy.wait_send()
        self.sent = []


def gather_flow(net, own, full, local_sem):
    z, h, c = net.z, net.h, net.c
    other_y, other_c = net.at(h=1 - h), net.at(c=1 - c)
    right, left = net.at(z=net.dz(1)), net.at(z=net.dz(-1))
    me = c * NZ + z
    ra, rb = pl.ds(0, HALF), pl.ds(HALF, HALF)
    a_first, a_last = pl.ds(0, QUART), pl.ds(QUART, QUART)
    b_first, b_last = pl.ds(HALF, QUART), pl.ds(HALF + QUART, QUART)
    core_sems = [net.new() for _ in range(NZ)]
    keep = pltpu.make_async_copy(own, full.at[me, h], local_sem)
    keep.start()
    ya = net.send(own.at[ra], full.at[me, h, ra], other_y)
    b_right = net.send(own.at[rb], full.at[me, h, rb], right)
    b_left = net.send(own.at[rb], full.at[me, h, rb], left)
    keep.wait()
    yb = [net.send(full.at[me, h, rb], full.at[me, h, rb], other_y)]

    def to_core(k, what):
        slot = c * NZ + net.dz(k)
        net.send(full.at[(slot,) + what], full.at[(slot,) + what], other_c, sem=core_sems[k % NZ])

    to_core(0, (h, slice(None)))
    both = slice(None)
    net.arrive(full.at[me, 1 - h, ra], ya)
    a_right = net.send(full.at[me, both, ra], full.at[me, both, ra], right)
    a_left = net.send(full.at[me, both, ra], full.at[me, both, ra], left)
    to_core(0, (1 - h, ra))
    yield
    pending = [(0, yb[0])]
    for k in range(4):
        zr, zl = c * NZ + net.dz(-1 - k), c * NZ + net.dz(1 + k)
        last, nxt_last = k == 3, k == 2
        br, bl = (b_first, b_last) if last else (rb, rb)
        net.arrive(full.at[zr, h, br], b_right)
        if not last:
            rows = b_first if nxt_last else rb
            b_right = net.send(full.at[zr, h, rows], full.at[zr, h, rows], right)
        net.arrive(full.at[zl, h, bl], b_left)
        if not last:
            rows = b_last if nxt_last else rb
            b_left = net.send(full.at[zl, h, rows], full.at[zl, h, rows], left)
        fresh = [(-1 - k, net.send(full.at[zr, h, rb], full.at[zr, h, rb], other_y))]
        to_core(-1 - k, (h, rb))
        if not last:
            fresh.append((1 + k, net.send(full.at[zl, h, rb], full.at[zl, h, rb], other_y)))
            to_core(1 + k, (h, rb))
        ar, al = (a_first, a_last) if last else (ra, ra)
        net.arrive(full.at[zr, both, ar], a_right)
        if not last:
            rows = a_first if nxt_last else ra
            a_right = net.send(full.at[zr, both, rows], full.at[zr, both, rows], right)
        net.arrive(full.at[zl, both, al], a_left)
        if not last:
            rows = a_last if nxt_last else ra
            a_left = net.send(full.at[zl, both, rows], full.at[zl, both, rows], left)
        to_core(-1 - k, (both, ra))
        if not last:
            to_core(1 + k, (both, ra))
        for d, sem in pending:
            slot = c * NZ + net.dz(d)
            net.arrive(full.at[slot, 1 - h, rb], sem)
            to_core(d, (1 - h, rb))
        pending = fresh
        yield
    for d, sem in pending:
        slot = c * NZ + net.dz(d)
        net.arrive(full.at[slot, 1 - h, rb], sem)
        to_core(d, (1 - h, rb))
    for k in range(NZ):
        net.arrive(full.at[(1 - c) * NZ + net.dz(k)], core_sems[k])
    yield


def small_gather(net, own, full, local_sem):
    z, h, c = net.z, net.h, net.c
    right, left = net.at(z=net.dz(1)), net.at(z=net.dz(-1))
    me = c * NZ + z
    keep = pltpu.make_async_copy(own, full.at[h, me], local_sem)
    keep.start()
    y = net.send(own, full.at[h, me], net.at(h=1 - h))
    keep.wait()
    net.arrive(full.at[1 - h, me], y)
    r = net.send(full.at[:, me], full.at[:, me], right)
    l = net.send(full.at[:, me], full.at[:, me], left)
    yield
    for k in range(4):
        zr, zl = c * NZ + net.dz(-1 - k), c * NZ + net.dz(1 + k)
        net.arrive(full.at[:, zr], r)
        if k < 3:
            r = net.send(full.at[:, zr], full.at[:, zr], right)
            net.arrive(full.at[:, zl], l)
            if k < 2:
                l = net.send(full.at[:, zl], full.at[:, zl], left)
        yield
    mine, theirs = pl.ds(pl.multiple_of(c * NZ, NZ), NZ), pl.ds(pl.multiple_of((1 - c) * NZ, NZ), NZ)
    i = net.send(full.at[:, mine], full.at[:, mine], net.at(c=1 - c))
    net.arrive(full.at[:, theirs], i)
    yield


def cols(xt, lo=None):
    if lo is None:
        return pl.ds(pl.multiple_of(xt * 256, 256), 256)
    return pl.ds(pl.multiple_of(xt * 256 + lo * 128, 128), 128)


def reduce_flow(net, part, out, hop_r, hop_l, in_r, in_l, y_out, y_in):
    x, lo = net.x, net.lo
    right, left = net.at(x=net.dx(1)), net.at(x=net.dx(-1))
    n = ROWS // 2
    r0, r1 = pl.ds(0, n), pl.ds(n, n)
    far, nr, nl, own = cols(net.dx(2)), cols(net.dx(1)), cols(net.dx(-1)), cols(x)
    s1 = net.send(part.at[r0, far], hop_r, right)
    s2 = net.send(part.at[r1, far], hop_l, left)
    yield
    s3 = net.send(part.at[r1, nr], in_r.at[r1], right)
    s4 = net.send(part.at[r0, nl], in_l.at[r0], left)
    yield
    tile = 160

    def add(dst_rows, where, src):
        def body(i, carry):
            at = pl.multiple_of(i * tile, tile)
            rows = pl.ds(pl.multiple_of(dst_rows + at, tile), tile)
            part[rows, where] = (
                part[rows, where].astype(F32) + src[pl.ds(at, tile), :].astype(F32)
            ).astype(BF)
            return carry

        lax.fori_loop(0, n // tile, body, 0)

    net.arrive(hop_r, s1)
    add(0, nr, hop_r)
    s5 = net.send(part.at[r0, nr], in_r.at[r0], right)
    net.arrive(hop_l, s2)
    add(n, nl, hop_l)
    s6 = net.send(part.at[r1, nl], in_l.at[r1], left)
    yield
    waits = {0: ((in_r, s5), (in_l, s4)), 1: ((in_r, s3), (in_l, s6))}
    ys = []
    for half in (1, 0):
        rows_half = (r0, r1)[half]
        for buf, sem in waits[half]:
            net.arrive(buf.at[rows_half], sem)

        def total(i, carry):
            rows = pl.ds(pl.multiple_of(half * n + i * tile, tile), tile)
            for side, keep in ((lo, True), (1 - lo, False)):
                inner = pl.ds(pl.multiple_of(side * 128, 128), 128)
                acc = (
                    part[rows, cols(x, side)].astype(F32)
                    + in_r[rows, inner].astype(F32)
                    + in_l[rows, inner].astype(F32)
                )
                if keep:
                    out[rows, :] = acc
                else:
                    y_out[rows, :] = acc.astype(BF)
            return carry

        lax.fori_loop(0, n // tile, total, 0)
        ys.append((half, net.send(y_out.at[rows_half], y_in.at[rows_half], net.at(lo=1 - lo))))
        yield
    for half, sem in ys:
        net.arrive(y_in.at[(r0, r1)[half]], sem)

        def last(i, carry):
            rows = pl.ds(pl.multiple_of(half * n + i * tile, tile), tile)
            out[rows, :] = out[rows, :] + y_in[rows, :].astype(F32)
            return carry

        lax.fori_loop(0, n // tile, last, 0)
    yield


def run_together(*flows):
    flows = list(flows)
    while flows:
        for flow in list(flows):
            try:
                next(flow)
            except StopIteration:
                flows.remove(flow)


def ranks(info, expert, tri, rank_ref, weight_ref):
    for side in range(2):
        hit = info[side, :, 0:8, :] == expert[...][0:1, :][None]
        mask = jnp.max(jnp.where(hit, 1.0, 0.0), axis=1)
        weight = jnp.sum(jnp.where(hit, info[side, :, 8:16, :], 0.0), axis=1)
        before = jnp.dot(mask.astype(BF), tri[...], preferred_element_type=F32)
        where = pl.ds(side * TOK, TOK)
        rank_ref[:, where] = jnp.where(mask > 0.5, before + float(side * CAP), -1.0)
        weight_ref[:, where] = weight


def picker(rank_ref, p):
    slots = lax.broadcasted_iota(jnp.int32, (PAIR, 2 * TOK), 0).astype(F32)
    return jnp.where(slots == rank_ref[pl.ds(p, 1), :], 1.0, 0.0)


def dispatch_kernel(
    tok, cot, info, wg, wd, eold, enew, tri,
    hid_o, slope_o, rows_new, cot_new, rank_old, weight_old,
    tok_all, cot_all, info_all, rows, part_a, part_b, acc_a, acc_b,
    hop_r, hop_l, in_r, in_l, y_out, y_in,
    rank_new, weight_new,
    local_sem, send_sem, recv_sem,
):
    net = Links(send_sem, recv_sem)
    net.barrier()
    small = small_gather(net, info, info_all, local_sem.at[0])
    toks = gather_flow(net, tok, tok_all, local_sem.at[1])
    cots = gather_flow(net, cot, cot_all, local_sem.at[2])
    run_together(small, toks)
    next(cots)
    ranks(info_all, eold, tri, rank_old, weight_old)
    ranks(info_all, enew, tri, rank_new, weight_new)
    next(cots)

    def pick_tok(p, carry):
        block = tok_all[p].reshape(2 * TOK, tok_all.shape[-1])
        at = pl.ds(pl.multiple_of(p * PAIR, 16), PAIR)
        for rank_ref, out in ((rank_old, rows), (rank_new, rows_new)):
            sel = picker(rank_ref, p).astype(BF)
            out[at, :] = jnp.dot(sel, block, preferred_element_type=F32).astype(BF)
        return carry

    def pick_cot(p, carry):
        block = cot_all[p].reshape(2 * TOK, cot_all.shape[-1])
        at = pl.ds(pl.multiple_of(p * PAIR, 16), PAIR)
        for rank_ref, weight_ref, out in ((rank_old, weight_old, rows), (rank_new, weight_new, cot_new)):
            hit = picker(rank_ref, p)
            weight = jnp.sum(hit * weight_ref[pl.ds(p, 1), :], axis=1, keepdims=True)
            sel = jnp.dot(hit.astype(BF), block, preferred_element_type=F32)
            out[at, :] = (sel * weight).astype(BF)
        return carry

    def project(w, part, shift):
        where = cols(net.dx(shift))
        tile = 320

        def body(i, carry):
            at = pl.ds(pl.multiple_of(i * tile, tile), tile)
            part[at, where] = lax.dot_general(
                rows[at, :], w[where, :], (((1,), (1,)), ((), ())), preferred_element_type=F32
            ).astype(BF)
            return carry

        lax.fori_loop(0, ROWS // tile, body, 0)

    def flow(w, part, out, bufs):
        project(w, part, 2)
        red = reduce_flow(net, part, out, *bufs)
        next(red)
        project(w, part, 1)
        project(w, part, -1)
        next(red)
        project(w, part, 0)
        yield
        yield from red

    bufs_a = [r.at[0] for r in (hop_r, hop_l, in_r, in_l, y_out, y_in)]
    bufs_b = [r.at[1] for r in (hop_r, hop_l, in_r, in_l, y_out, y_in)]
    lax.fori_loop(0, 16, pick_tok, 0)
    next(cots)
    run_together(flow(wg, part_a, acc_a, bufs_a), cots)
    lax.fori_loop(0, 16, pick_cot, 0)
    run_together(flow(wd, part_b, acc_b, bufs_b))

    def act(i, carry):
        at = pl.ds(pl.multiple_of(i * 160, 160), 160)
        pre, back = acc_a[at, :], acc_b[at, :]
        sig = jax.nn.sigmoid(pre)
        hid_o[at, :] = (pre * sig).astype(BF)
        slope_o[at, :] = (back * sig * (1.0 + pre * (1.0 - sig))).astype(BF)
        return carry

    lax.fori_loop(0, ROWS // 160, act, 0)
    net.drain()


def dispatch(tokens, cotangent, info, w_gate, w_down, eold, enew, tri):
    width = tokens.shape[1]
    vm = pl.BlockSpec(memory_space=pltpu.VMEM)
    sds = jax.ShapeDtypeStruct
    half = ROWS // 2
    return pl.pallas_call(
        dispatch_kernel,
        out_shape=(
            sds((ROWS, 128), BF),
            sds((ROWS, 128), BF),
            sds((ROWS, width), BF),
            sds((ROWS, width), BF),
            sds((16, 256), F32),
            sds((16, 256), F32),
        ),
        in_specs=[vm] * 8,
        out_specs=(vm,) * 6,
        scratch_shapes=[
            pltpu.VMEM((16, 2, TOK, width), BF),
            pltpu.VMEM((16, 2, TOK, width), BF),
            pltpu.VMEM((2, 16, 16, 128), F32),
            pltpu.VMEM((ROWS, width), BF),
            pltpu.VMEM((ROWS, 1024), BF),
            pltpu.VMEM((ROWS, 1024), BF),
            pltpu.VMEM((ROWS, 128), F32),
            pltpu.VMEM((ROWS, 128), F32),
            pltpu.VMEM((2, half, 256), BF),
            pltpu.VMEM((2, half, 256), BF),
            pltpu.VMEM((2, ROWS, 256), BF),
            pltpu.VMEM((2, ROWS, 256), BF),
            pltpu.VMEM((2, ROWS, 128), BF),
            pltpu.VMEM((2, ROWS, 128), BF),
            pltpu.VMEM((16, 256), F32),
            pltpu.VMEM((16, 256), F32),
            pltpu.SemaphoreType.DMA((3,)),
            pltpu.SemaphoreType.DMA((192,)),
            pltpu.SemaphoreType.DMA((192,)),
        ],
        compiler_params=pltpu.CompilerParams(
            collective_id=0, has_side_effects=True, vmem_limit_bytes=VMEM_LIMIT
        ),
    )(tokens, cotangent, info, w_gate, w_down, eold, enew, tri)


N1 = 704


def whole_flow(net, own, full, local_sem):
    x, lo = net.x, net.lo
    right, left, other = net.at(x=net.dx(1)), net.at(x=net.dx(-1)), net.at(lo=1 - lo)
    n2 = ROWS - N1
    p, q = pl.ds(0, N1), pl.ds(N1, n2)
    p0, p1 = pl.ds(0, N1 // 2), pl.ds(N1 // 2, N1 // 2)
    q0, q1 = pl.ds(N1, n2 // 2), pl.ds(N1 + n2 // 2, n2 // 2)
    mine = cols(x, lo)
    keep = pltpu.make_async_copy(own, full.at[:, mine], local_sem)
    keep.start()
    y = net.send(own.at[p], full.at[p, mine], other)
    qr = net.send(own.at[q], full.at[q, mine], right)
    ql = net.send(own.at[q], full.at[q, mine], left)
    ys = [(x, net.send(own.at[q], full.at[q, mine], other))]
    keep.wait()
    yield
    net.arrive(full.at[p, cols(x, 1 - lo)], y)
    pr = net.send(full.at[p, cols(x)], full.at[p, cols(x)], right)
    pls = net.send(full.at[p, cols(x)], full.at[p, cols(x)], left)
    yield
    xl, xr, xf = net.dx(-1), net.dx(1), net.dx(2)

    def fwd(rows, where, peer):
        return net.send(full.at[rows, where], full.at[rows, where], peer)

    net.arrive(full.at[q, cols(xl, lo)], qr)
    q2r = fwd(q0, cols(xl, lo), right)
    ys.append((xl, fwd(q, cols(xl, lo), other)))
    net.arrive(full.at[q, cols(xr, lo)], ql)
    q2l = fwd(q1, cols(xr, lo), left)
    ys.append((xr, fwd(q, cols(xr, lo), other)))
    yield
    net.arrive(full.at[p, cols(xl)], pr)
    p2r = fwd(p0, cols(xl), right)
    net.arrive(full.at[p, cols(xr)], pls)
    p2l = fwd(p1, cols(xr), left)
    yield
    net.arrive(full.at[q0, cols(xf, lo)], q2r)
    net.arrive(full.at[q1, cols(xf, lo)], q2l)
    ys.append((xf, fwd(q, cols(xf, lo), other)))
    yield
    net.arrive(full.at[p0, cols(xf)], p2r)
    net.arrive(full.at[p1, cols(xf)], p2l)
    for xt, sem in ys:
        net.arrive(full.at[q, cols(xt, 1 - lo)], sem)
    yield


def move_flow(net, hid_s, slope_s, src_z, src_hc, spread, picked, moved, local_sems):
    z, h, c = net.z, net.h, net.c
    n = ROWS // NZ
    hc = h * 2 + c
    sems = []
    keeps = []
    for k in range(NZ):
        zt = net.dz(k)
        rows = pl.ds(pl.multiple_of(zt * n, n), n)
        for m, src in enumerate((hid_s, slope_s)):
            if k == 0:
                copy = pltpu.make_async_copy(src.at[rows], spread.at[z, hc, m], local_sems.at[m])
                copy.start()
                keeps.append(copy)
            else:
                sems.append((-k, m, net.send(src.at[rows], spread.at[z, hc, m], net.at(z=zt))))
    for copy in keeps:
        copy.wait()
    yield
    for k, m, sem in sems:
        net.arrive(spread.at[net.dz(k), hc, m], sem)
    s = net.send(spread.at[:, hc], spread.at[:, hc], net.at(h=1 - h))
    t = net.send(spread.at[:, hc], spread.at[:, hc], net.at(c=1 - c))
    yield
    net.arrive(spread.at[:, (1 - h) * 2 + c], s)
    u = net.send(spread.at[:, (1 - h) * 2 + c], spread.at[:, (1 - h) * 2 + c], net.at(c=1 - c))
    net.arrive(spread.at[:, h * 2 + 1 - c], t)
    net.arrive(spread.at[:, (1 - h) * 2 + 1 - c], u)

    def pick(i, carry):
        picked[i] = spread[src_z[i], src_hc[i]]
        return carry

    lax.fori_loop(0, NZ, pick, 0)
    yield
    sems, keeps = [], []
    mine = pl.ds(pl.multiple_of(z * n, n), n)
    for k in range(NZ):
        zt = net.dz(k)
        for m in range(2):
            if k == 0:
                copy = pltpu.make_async_copy(picked.at[z, m], moved.at[m, mine], local_sems.at[m])
                copy.start()
                keeps.append(copy)
            else:
                sems.append((-k, m, net.send(picked.at[zt, m], moved.at[m, mine], net.at(z=zt))))
    for copy in keeps:
        copy.wait()
    yield
    for k, m, sem in sems:
        net.arrive(moved.at[m, pl.ds(pl.multiple_of(net.dz(k) * n, n), n)], sem)
    yield


def add_into(dst, *srcs):
    lead, rows = dst.shape[:-2], dst.shape[-2]

    def body(i, carry):
        at = pl.ds(pl.multiple_of(i * 16, 16), 16)
        for j in range(lead[0] if lead else 1):
            where = (j, at) if lead else (at,)
            acc = dst[where].astype(F32)
            for src in srcs:
                acc = acc + src[where].astype(F32)
            dst[where] = acc.astype(BF)
        return carry

    lax.fori_loop(0, rows // 16, body, 0)


def return_flow(net, contribution, to_core, from_core, sums, y_b, ring_ra, ring_la, ring_rb, ring_lb, y_a, out):
    z, h, c = net.z, net.h, net.c
    width = out.shape[-1]
    other_y, other_c = net.at(h=1 - h), net.at(c=1 - c)
    right, left = net.at(z=net.dz(1)), net.at(z=net.dz(-1))
    ra, rb = pl.ds(0, HALF), pl.ds(HALF, HALF)
    a_first, a_last = pl.ds(0, QUART), pl.ds(QUART, QUART)
    b_first, b_last = pl.ds(HALF, QUART), pl.ds(HALF + QUART, QUART)
    both = slice(None)
    core, yb = {}, {}
    for k in (4, 3, -3, 2, -2, 1, -1, 0):
        zt = net.dz(k)
        to_core[zt] = contribution((1 - c) * NZ + zt).astype(BF).reshape(2, TOK, width)
        core[k] = net.send(to_core.at[zt], from_core.at[zt], other_c)
    yield
    ar = al = br = bl = None
    for s in range(5):
        ks = (4,) if s == 0 else (0,) if s == 4 else (4 - s, s - 4)
        for k in ks:
            zt = net.dz(k)
            net.arrive(from_core.at[zt], core[k])
            got = from_core[zt].astype(F32).reshape(2 * TOK, width)
            sums[zt] = (contribution(c * NZ + zt) + got).astype(BF).reshape(2, TOK, width)
            yb[k] = net.send(sums.at[zt, 1 - h, rb], y_b.at[zt], other_y)
        zr, zl = net.dz(4 - s), net.dz(s - 4)
        if s == 0:
            ar = net.send(sums.at[zr, both, a_first], ring_ra.at[0, both, a_first], right)
            al = net.send(sums.at[zr, both, a_last], ring_la.at[0, both, a_last], left)
            net.arrive(y_b.at[zr], yb[4])
            add_into(sums.at[zr, h, rb], y_b.at[zr])
            br = net.send(sums.at[zr, h, b_first], ring_rb.at[0, a_first], right)
            bl = net.send(sums.at[zr, h, b_last], ring_lb.at[0, a_last], left)
            yield
            continue
        at_r, at_l = (a_first, a_last) if s == 1 else (ra, ra)
        bt_r, bt_l = (b_first, b_last) if s == 1 else (rb, rb)
        if s < 4:
            net.arrive(ring_ra.at[s - 1, both, at_r], ar)
            add_into(sums.at[zr, both, at_r], ring_ra.at[s - 1, both, at_r])
            ar = net.send(sums.at[zr, both, ra], ring_ra.at[s], right)
            net.arrive(ring_la.at[s - 1, both, at_l], al)
            add_into(sums.at[zl, both, at_l], ring_la.at[s - 1, both, at_l])
            al = net.send(sums.at[zl, both, ra], ring_la.at[s], left)
            for k in ks:
                net.arrive(y_b.at[net.dz(k)], yb[k])
                add_into(sums.at[net.dz(k), h, rb], y_b.at[net.dz(k)])
            net.arrive(ring_rb.at[s - 1, at_r], br)
            add_into(sums.at[zr, h, bt_r], ring_rb.at[s - 1, at_r])
            br = net.send(sums.at[zr, h, rb], ring_rb.at[s], right)
            net.arrive(ring_lb.at[s - 1, at_l], bl)
            add_into(sums.at[zl, h, bt_l], ring_lb.at[s - 1, at_l])
            bl = net.send(sums.at[zl, h, rb], ring_lb.at[s], left)
            yield
            continue
        net.arrive(ring_ra.at[3], ar)
        net.arrive(ring_la.at[3], al)
        add_into(sums.at[z, both, ra], ring_ra.at[3], ring_la.at[3])
        ya = net.send(sums.at[z, 1 - h, ra], y_a, other_y)
        net.arrive(y_b.at[z], yb[0])
        net.arrive(ring_rb.at[3], br)
        net.arrive(ring_lb.at[3], bl)
        out[rb, :] = (
            sums[z, h, rb, :].astype(F32)
            + y_b[z].astype(F32)
            + ring_rb[3].astype(F32)
            + ring_lb[3].astype(F32)
        ).astype(BF)
        yield
        net.arrive(y_a, ya)
        out[ra, :] = (sums[z, h, ra, :].astype(F32) + y_a[...].astype(F32)).astype(BF)
    yield


def finish_kernel(
    hid_s, slope_s, rows_new, cot_new, rank, weight, wg, wd, src_z, src_hc,
    layer_out, token_grads, grad_gate, grad_down,
    hidden, slope, hidden_new, slope_new, spread, picked, moved, out_rows, back_rows,
    to_core, from_core, sums, y_b, ring_ra, ring_la, ring_rb, ring_lb, y_a,
    local_sem, send_sem, recv_sem,
):
    net = Links(send_sem, recv_sem)
    net.barrier(all_z=True)
    whole_h = whole_flow(net, hid_s, hidden, local_sem.at[0])
    whole_s = whole_flow(net, slope_s, slope, local_sem.at[1])
    move = move_flow(net, hid_s, slope_s, src_z, src_hc, spread, picked, moved, local_sem.at[pl.ds(2, 2)])

    def weighted(i, carry):
        at = pl.ds(pl.multiple_of(i * PAIR, 16), PAIR)
        w = jnp.sum(picker(rank, i) * weight[pl.ds(i, 1), :], axis=1, keepdims=True)
        out = jnp.dot(hidden[at, :], wd[...], preferred_element_type=F32)
        out_rows[at, :] = (out * w).astype(BF)
        return carry

    def plain(i, carry):
        at = pl.ds(pl.multiple_of(i * 160, 160), 160)
        back_rows[at, :] = jnp.dot(slope[at, :], wg[...], preferred_element_type=F32).astype(BF)
        return carry

    def placed(rows):
        def contribution(p):
            sel = picker(rank, p).astype(BF)
            at = pl.ds(pl.multiple_of(p * PAIR, 16), PAIR)
            return lax.dot_general(sel, rows[at, :], (((0,), (0,)), ((), ())), preferred_element_type=F32)

        return contribution

    def outer(left, right, out):
        def body(i, carry):
            at = pl.ds(pl.multiple_of(i * 128, 128), 128)
            out[at, :] = lax.dot_general(
                left[:, at], right[...], (((0,), (0,)), ((), ())), preferred_element_type=F32
            ).astype(BF)
            return carry

        lax.fori_loop(0, 8, body, 0)

    bufs = (to_core, from_core, sums, y_b, ring_ra, ring_la, ring_rb, ring_lb, y_a)

    def forward():
        yield from whole_h
        lax.fori_loop(0, 16, weighted, 0)
        yield from return_flow(net, placed(out_rows), *[b.at[0] for b in bufs], layer_out)

    def backward():
        yield from whole_s
        lax.fori_loop(0, ROWS // 160, plain, 0)
        yield from return_flow(net, placed(back_rows), *[b.at[1] for b in bufs], token_grads)

    def grads():
        yield from move
        first = whole_flow(net, moved.at[1], slope_new, local_sem.at[0])
        second = whole_flow(net, moved.at[0], hidden_new, local_sem.at[1])
        next(first)
        next(second)
        for _ in range(5):
            next(first)
            next(second)
            yield
        outer(slope_new, rows_new, grad_gate)
        yield
        outer(hidden_new, cot_new, grad_down)
        yield

    run_together(forward(), backward(), grads())
    net.drain()


def finish(*args):
    width = args[2].shape[1]
    vm = pl.BlockSpec(memory_space=pltpu.VMEM)
    sm = pl.BlockSpec(memory_space=pltpu.SMEM)
    sds = jax.ShapeDtypeStruct
    n = ROWS // NZ
    return pl.pallas_call(
        finish_kernel,
        out_shape=(
            sds((TOK, width), BF),
            sds((TOK, width), BF),
            sds((1024, width), BF),
            sds((1024, width), BF),
        ),
        in_specs=[vm] * 8 + [sm] * 2,
        out_specs=(vm,) * 4,
        scratch_shapes=[
            pltpu.VMEM((ROWS, 1024), BF),
            pltpu.VMEM((ROWS, 1024), BF),
            pltpu.VMEM((ROWS, 1024), BF),
            pltpu.VMEM((ROWS, 1024), BF),
            pltpu.VMEM((NZ, 4, 2, n, 128), BF),
            pltpu.VMEM((NZ, 2, n, 128), BF),
            pltpu.VMEM((2, ROWS, 128), BF),
            pltpu.VMEM((ROWS, width), BF),
            pltpu.VMEM((ROWS, width), BF),
            pltpu.VMEM((2, NZ, 2, TOK, width), BF),
            pltpu.VMEM((2, NZ, 2, TOK, width), BF),
            pltpu.VMEM((2, NZ, 2, TOK, width), BF),
            pltpu.VMEM((2, NZ, HALF, width), BF),
            pltpu.VMEM((2, 4, 2, HALF, width), BF),
            pltpu.VMEM((2, 4, 2, HALF, width), BF),
            pltpu.VMEM((2, 4, HALF, width), BF),
            pltpu.VMEM((2, 4, HALF, width), BF),
            pltpu.VMEM((2, HALF, width), BF),
            pltpu.SemaphoreType.DMA((4,)),
            pltpu.SemaphoreType.DMA((256,)),
            pltpu.SemaphoreType.DMA((256,)),
        ],
        compiler_params=pltpu.CompilerParams(
            collective_id=1, has_side_effects=True, vmem_limit_bytes=VMEM_LIMIT
        ),
    )(*args)


def per_device(tokens, cotangent, expert_ids, gate_weights, owner_old, owner_new, w_gate, w_down):
    me = lax.axis_index("expert")
    labels = jnp.arange(32, dtype=jnp.int32)
    info = jnp.concatenate([expert_ids.T.astype(F32), gate_weights.T], axis=0)
    eold = jnp.broadcast_to(jnp.sum(jnp.where(owner_old == me, labels, 0)).astype(F32), (8, 128))
    enew = jnp.broadcast_to(jnp.sum(jnp.where(owner_new == me, labels, 0)).astype(F32), (8, 128))
    lane = jnp.arange(128)
    tri = (lane[:, None] < lane[None, :]).astype(BF)
    targets = jnp.arange(NZ, dtype=jnp.int32) * 4 + me % 4
    source = jnp.sum(jnp.where(owner_new[None, :] == targets[:, None], owner_old[None, :], 0), axis=1)
    gate_here, down_here = w_gate[0], w_down[0]
    hid_s, slope_s, rows_new, cot_new, rank, weight = dispatch(
        tokens, cotangent, info, gate_here, down_here, eold, enew, tri
    )
    layer_out, token_grads, grad_gate, grad_down = finish(
        hid_s, slope_s, rows_new, cot_new, rank, weight, gate_here, down_here, source // 4, source % 4
    )
    return (layer_out, token_grads, grad_gate[None], grad_down[None])


def solution(mesh):
    return jax.shard_map(
        per_device,
        mesh=mesh,
        in_specs=(
            P("expert", "hid"),
            P("expert", "hid"),
            P("expert", None),
            P("expert", None),
            P(),
            P(),
            P("expert", None, "hid"),
            P("expert", None, "hid"),
        ),
        out_specs=(
            P("expert", "hid"),
            P("expert", "hid"),
            P("expert", None, "hid"),
            P("expert", None, "hid"),
        ),
        check_vma=False,
    )
```

```python
import functools

import jax
import jax.numpy as jnp
from jax import lax
from jax.experimental import pallas as pl
from jax.experimental.pallas import tpu as pltpu
from jax.sharding import PartitionSpec as P

MESH = pl.DeviceIdType.MESH
BF = jnp.bfloat16
F32 = jnp.float32
VMEM_LIMIT = 62 << 20
NZ, CAP, TOK, HALF, QUART = 8, 40, 128, 64, 32
ROWS, PAIR = 1280, 80


def place():
    e, d = lax.axis_index("expert"), lax.axis_index("hid")
    return e // 4, (e // 2) % 2, e % 2, d // 4, d % 4


class Links:
    def __init__(self, send_sem, recv_sem):
        self.z, self.h, self.c, self.lo, self.x = place()
        self.send_sem, self.recv_sem, self.used, self.sent = send_sem, recv_sem, 0, []

    def at(self, z=None, h=None, c=None, lo=None, x=None):
        z = self.z if z is None else z
        h = self.h if h is None else h
        c = self.c if c is None else c
        lo = self.lo if lo is None else lo
        x = self.x if x is None else x
        return (z * 4 + h * 2 + c, lo * 4 + x)

    def dz(self, k):
        return (self.z + k + NZ) % NZ

    def dx(self, k):
        return (self.x + k + 4) % 4

    def barrier(self):
        peers = [self.at(z=self.dz(k)) for k in range(1, NZ)]
        peers += [
            self.at(h=1 - self.h),
            self.at(c=1 - self.c),
            self.at(x=self.dx(1)),
            self.at(x=self.dx(-1)),
            self.at(lo=1 - self.lo),
        ]
        sem = pltpu.get_barrier_semaphore()
        for peer in peers:
            pl.semaphore_signal(sem, inc=1, device_id=peer, device_id_type=MESH)
        pl.semaphore_wait(sem, len(peers))

    def new(self):
        self.used += 1
        return self.used - 1

    def send(self, src, dst, peer, sem=None):
        i = self.new()
        copy = pltpu.make_async_remote_copy(
            src_ref=src,
            dst_ref=dst,
            send_sem=self.send_sem.at[i],
            recv_sem=self.recv_sem.at[i if sem is None else sem],
            device_id=peer,
            device_id_type=MESH,
        )
        copy.start()
        self.sent.append(copy)
        return i

    def arrive(self, ref, i):
        pltpu.make_async_copy(ref, ref, self.recv_sem.at[i]).wait()

    def drain(self):
        for copy in self.sent:
            copy.wait_send()
        self.sent = []


def gather_flow(net, own, full, local_sem):
    z, h, c = net.z, net.h, net.c
    other_y, other_c = net.at(h=1 - h), net.at(c=1 - c)
    right, left = net.at(z=net.dz(1)), net.at(z=net.dz(-1))
    me = c * NZ + z
    ra, rb = pl.ds(0, HALF), pl.ds(HALF, HALF)
    a_first, a_last = pl.ds(0, QUART), pl.ds(QUART, QUART)
    b_first, b_last = pl.ds(HALF, QUART), pl.ds(HALF + QUART, QUART)
    core_sems = [net.new() for _ in range(NZ)]
    keep = pltpu.make_async_copy(own, full.at[me, h], local_sem)
    keep.start()
    ya = net.send(own.at[ra], full.at[me, h, ra], other_y)
    b_right = net.send(own.at[rb], full.at[me, h, rb], right)
    b_left = net.send(own.at[rb], full.at[me, h, rb], left)
    keep.wait()
    yb = [net.send(full.at[me, h, rb], full.at[me, h, rb], other_y)]

    def to_core(k, what):
        slot = c * NZ + net.dz(k)
        net.send(full.at[(slot,) + what], full.at[(slot,) + what], other_c, sem=core_sems[k % NZ])

    to_core(0, (h, slice(None)))
    both = slice(None)
    net.arrive(full.at[me, 1 - h, ra], ya)
    a_right = net.send(full.at[me, both, ra], full.at[me, both, ra], right)
    a_left = net.send(full.at[me, both, ra], full.at[me, both, ra], left)
    to_core(0, (1 - h, ra))
    yield
    pending = [(0, yb[0])]
    for k in range(4):
        zr, zl = c * NZ + net.dz(-1 - k), c * NZ + net.dz(1 + k)
        last, nxt_last = k == 3, k == 2
        br, bl = (b_first, b_last) if last else (rb, rb)
        net.arrive(full.at[zr, h, br], b_right)
        if not last:
            rows = b_first if nxt_last else rb
            b_right = net.send(full.at[zr, h, rows], full.at[zr, h, rows], right)
        net.arrive(full.at[zl, h, bl], b_left)
        if not last:
            rows = b_last if nxt_last else rb
            b_left = net.send(full.at[zl, h, rows], full.at[zl, h, rows], left)
        fresh = [(-1 - k, net.send(full.at[zr, h, rb], full.at[zr, h, rb], other_y))]
        to_core(-1 - k, (h, rb))
        if not last:
            fresh.append((1 + k, net.send(full.at[zl, h, rb], full.at[zl, h, rb], other_y)))
            to_core(1 + k, (h, rb))
        ar, al = (a_first, a_last) if last else (ra, ra)
        net.arrive(full.at[zr, both, ar], a_right)
        if not last:
            rows = a_first if nxt_last else ra
            a_right = net.send(full.at[zr, both, rows], full.at[zr, both, rows], right)
        net.arrive(full.at[zl, both, al], a_left)
        if not last:
            rows = a_last if nxt_last else ra
            a_left = net.send(full.at[zl, both, rows], full.at[zl, both, rows], left)
        to_core(-1 - k, (both, ra))
        if not last:
            to_core(1 + k, (both, ra))
        for d, sem in pending:
            slot = c * NZ + net.dz(d)
            net.arrive(full.at[slot, 1 - h, rb], sem)
            to_core(d, (1 - h, rb))
        pending = fresh
        yield
    for d, sem in pending:
        slot = c * NZ + net.dz(d)
        net.arrive(full.at[slot, 1 - h, rb], sem)
        to_core(d, (1 - h, rb))
    for k in range(NZ):
        net.arrive(full.at[(1 - c) * NZ + net.dz(k)], core_sems[k])
    yield


def small_gather(net, own, full, local_sem):
    z, h, c = net.z, net.h, net.c
    right, left = net.at(z=net.dz(1)), net.at(z=net.dz(-1))
    me = c * NZ + z
    keep = pltpu.make_async_copy(own, full.at[h, me], local_sem)
    keep.start()
    y = net.send(own, full.at[h, me], net.at(h=1 - h))
    keep.wait()
    net.arrive(full.at[1 - h, me], y)
    r = net.send(full.at[:, me], full.at[:, me], right)
    l = net.send(full.at[:, me], full.at[:, me], left)
    yield
    for k in range(4):
        zr, zl = c * NZ + net.dz(-1 - k), c * NZ + net.dz(1 + k)
        net.arrive(full.at[:, zr], r)
        if k < 3:
            r = net.send(full.at[:, zr], full.at[:, zr], right)
            net.arrive(full.at[:, zl], l)
            if k < 2:
                l = net.send(full.at[:, zl], full.at[:, zl], left)
        yield
    mine, theirs = pl.ds(pl.multiple_of(c * NZ, NZ), NZ), pl.ds(pl.multiple_of((1 - c) * NZ, NZ), NZ)
    i = net.send(full.at[:, mine], full.at[:, mine], net.at(c=1 - c))
    net.arrive(full.at[:, theirs], i)
    yield


def cols(xt, lo=None):
    if lo is None:
        return pl.ds(pl.multiple_of(xt * 256, 256), 256)
    return pl.ds(pl.multiple_of(xt * 256 + lo * 128, 128), 128)


def reduce_flow(net, part, out, hop_r, hop_l, in_r, in_l, y_out, y_in):
    x, lo = net.x, net.lo
    right, left = net.at(x=net.dx(1)), net.at(x=net.dx(-1))
    n = ROWS // 2
    r0, r1 = pl.ds(0, n), pl.ds(n, n)
    far, nr, nl, own = cols(net.dx(2)), cols(net.dx(1)), cols(net.dx(-1)), cols(x)
    s1 = net.send(part.at[r0, far], hop_r, right)
    s2 = net.send(part.at[r1, far], hop_l, left)
    yield
    s3 = net.send(part.at[r1, nr], in_r.at[r1], right)
    s4 = net.send(part.at[r0, nl], in_l.at[r0], left)
    yield
    tile = 160

    def add(dst_rows, where, src):
        def body(i, carry):
            at = pl.multiple_of(i * tile, tile)
            rows = pl.ds(pl.multiple_of(dst_rows + at, tile), tile)
            part[rows, where] = (
                part[rows, where].astype(F32) + src[pl.ds(at, tile), :].astype(F32)
            ).astype(BF)
            return carry

        lax.fori_loop(0, n // tile, body, 0)

    net.arrive(hop_r, s1)
    add(0, nr, hop_r)
    s5 = net.send(part.at[r0, nr], in_r.at[r0], right)
    net.arrive(hop_l, s2)
    add(n, nl, hop_l)
    s6 = net.send(part.at[r1, nl], in_l.at[r1], left)
    yield
    waits = {0: ((in_r, s5), (in_l, s4)), 1: ((in_r, s3), (in_l, s6))}
    ys = []
    for half in (1, 0):
        rows_half = (r0, r1)[half]
        for buf, sem in waits[half]:
            net.arrive(buf.at[rows_half], sem)

        def total(i, carry):
            rows = pl.ds(pl.multiple_of(half * n + i * tile, tile), tile)
            for side, keep in ((lo, True), (1 - lo, False)):
                inner = pl.ds(pl.multiple_of(side * 128, 128), 128)
                acc = (
                    part[rows, cols(x, side)].astype(F32)
                    + in_r[rows, inner].astype(F32)
                    + in_l[rows, inner].astype(F32)
                )
                if keep:
                    out[rows, :] = acc
                else:
                    y_out[rows, :] = acc.astype(BF)
            return carry

        lax.fori_loop(0, n // tile, total, 0)
        ys.append((half, net.send(y_out.at[rows_half], y_in.at[rows_half], net.at(lo=1 - lo))))
        yield
    for half, sem in ys:
        net.arrive(y_in.at[(r0, r1)[half]], sem)

        def last(i, carry):
            rows = pl.ds(pl.multiple_of(half * n + i * tile, tile), tile)
            out[rows, :] = out[rows, :] + y_in[rows, :].astype(F32)
            return carry

        lax.fori_loop(0, n // tile, last, 0)


def together(*flows):
    flows = list(flows)
    while flows:
        for flow in list(flows):
            try:
                next(flow)
            except StopIteration:
                flows.remove(flow)
        yield


def run_together(*flows):
    for _ in together(*flows):
        pass


def later(turns, flow):
    for _ in range(turns):
        yield
    yield from flow


def whole_flow(net, own, full, local_sem):
    x, lo = net.x, net.lo
    n = ROWS // 2
    right, left, other = net.at(x=net.dx(1)), net.at(x=net.dx(-1)), net.at(lo=1 - lo)
    h0, h1, rows = pl.ds(0, n), pl.ds(n, n), (pl.ds(0, n), pl.ds(n, n))
    mine = cols(x, lo)
    keep = pltpu.make_async_copy(own, full.at[:, mine], local_sem)
    keep.start()
    ys = [net.send(own.at[r], full.at[r, mine], other) for r in rows]
    keep.wait()
    yield

    def fwd(r, where, peer):
        return net.send(full.at[r, where], full.at[r, where], peer)

    one_r, one_l = [], []
    for r, y in zip(rows, ys):
        net.arrive(full.at[r, cols(x, 1 - lo)], y)
        one_r.append(fwd(r, cols(x), right))
        one_l.append(fwd(r, cols(x), left))
    yield
    xl, xr, xf = net.dx(-1), net.dx(1), net.dx(2)
    net.arrive(full.at[h0, cols(xl)], one_r[0])
    two_r = fwd(h0, cols(xl), right)
    net.arrive(full.at[h0, cols(xr)], one_l[0])
    yield
    net.arrive(full.at[h1, cols(xr)], one_l[1])
    two_l = fwd(h1, cols(xr), left)
    net.arrive(full.at[h1, cols(xl)], one_r[1])
    yield
    net.arrive(full.at[h0, cols(xf)], two_r)
    net.arrive(full.at[h1, cols(xf)], two_l)
    yield


def look_up(table, wanted, value):
    found = jnp.int32(0)
    for i in range(32):
        found = found + jnp.where(table[i] == wanted, value(i), 0)
    return found


def move_flow(net, shard, old, new, spread, picked, moved, local_sem):
    z, h, c = net.z, net.h, net.c
    n = ROWS // NZ
    hc, yc = h * 2 + c, (1 - h) * 2 + c
    far_first = (4, 3, -3, 2, -2, 1, -1)

    def eighth(zt):
        return pl.ds(pl.multiple_of(zt * n, n), n)

    keep = pltpu.make_async_copy(shard.at[eighth(z)], spread.at[z, hc], local_sem)
    keep.start()
    sems = []
    for k in far_first:
        zt = net.dz(k)
        sems.append((-k, net.send(shard.at[eighth(zt)], spread.at[z, hc], net.at(z=zt))))
    keep.wait()
    yield
    for k, sem in sems:
        net.arrive(spread.at[net.dz(k), hc], sem)
    s = net.send(spread.at[:, hc], spread.at[:, hc], net.at(h=1 - h))
    t = net.send(spread.at[:, hc], spread.at[:, hc], net.at(c=1 - c))
    yield
    net.arrive(spread.at[:, yc], s)
    u = net.send(spread.at[:, yc], spread.at[:, yc], net.at(c=1 - c))
    net.arrive(spread.at[:, h * 2 + 1 - c], t)
    net.arrive(spread.at[:, (1 - h) * 2 + 1 - c], u)

    def pick(i, carry):
        source = look_up(new, i * 4 + hc, lambda e: old[e])
        picked[i] = spread[source // 4, source % 4]
        return carry

    lax.fori_loop(0, NZ, pick, 0)
    keep = pltpu.make_async_copy(picked.at[z], moved.at[eighth(z)], local_sem)
    keep.start()
    sems = []
    for k in far_first:
        zt = net.dz(k)
        sems.append((-k, net.send(picked.at[zt], moved.at[eighth(z)], net.at(z=zt))))
    keep.wait()
    yield
    for k, sem in sems:
        net.arrive(moved.at[eighth(net.dz(k))], sem)
    yield


def ranks(info, expert, rank_ref, weight_ref):
    expert = expert.astype(F32)
    row = lax.broadcasted_iota(jnp.int32, (TOK, TOK), 0)
    tri = jnp.where(row < lax.broadcasted_iota(jnp.int32, (TOK, TOK), 1), 1.0, 0.0).astype(BF)
    for side in range(2):
        hit = info[side, :, 0:8, :] == expert
        mask = jnp.max(jnp.where(hit, 1.0, 0.0), axis=1)
        weight = jnp.sum(jnp.where(hit, info[side, :, 8:16, :], 0.0), axis=1)
        before = jnp.dot(mask.astype(BF), tri, preferred_element_type=F32)
        where = pl.ds(side * TOK, TOK)
        rank_ref[:, where] = jnp.where(mask > 0.5, before + float(side * CAP), -1.0)
        weight_ref[:, where] = weight


def picker(rank_ref, p):
    slots = lax.broadcasted_iota(jnp.int32, (PAIR, 2 * TOK), 0).astype(F32)
    return jnp.where(slots == rank_ref[pl.ds(p, 1), :], 1.0, 0.0)


def dispatch_kernel(
    tok, cot, info, wg, wd, old, new,
    slope_o, hidden, hid_moved, rows_new, cot_new, rank_old, weight_old,
    tok_all, cot_all, info_all, rows, part_a, part_b, acc_a, acc_b,
    hop_r, hop_l, in_r, in_l, y_out, y_in,
    rank_new, weight_new, hid_s, spread, picked,
    local_sem, send_sem, recv_sem,
):
    net = Links(send_sem, recv_sem)
    net.barrier()
    small = small_gather(net, info, info_all, local_sem.at[0])
    toks = gather_flow(net, tok, tok_all, local_sem.at[1])
    cots = later(2, gather_flow(net, cot, cot_all, local_sem.at[2]))
    for turn, _ in enumerate(together(small, toks)):
        if turn < 6:
            next(cots)
    me = net.z * 4 + net.h * 2 + net.c
    ranks(info_all, look_up(old, me, jnp.int32), rank_old, weight_old)
    ranks(info_all, look_up(new, me, jnp.int32), rank_new, weight_new)

    def pick_tok(p, carry):
        block = tok_all[p].reshape(2 * TOK, tok_all.shape[-1])
        at = pl.ds(pl.multiple_of(p * PAIR, 16), PAIR)
        for rank_ref, out in ((rank_old, rows), (rank_new, rows_new)):
            sel = picker(rank_ref, p).astype(BF)
            out[at, :] = jnp.dot(sel, block, preferred_element_type=F32).astype(BF)
        return carry

    def pick_cot(p, carry):
        block = cot_all[p].reshape(2 * TOK, cot_all.shape[-1])
        at = pl.ds(pl.multiple_of(p * PAIR, 16), PAIR)
        for rank_ref, weight_ref, out in ((rank_old, weight_old, rows), (rank_new, weight_new, cot_new)):
            hit = picker(rank_ref, p)
            weight = jnp.sum(hit * weight_ref[pl.ds(p, 1), :], axis=1, keepdims=True)
            sel = jnp.dot(hit.astype(BF), block, preferred_element_type=F32)
            out[at, :] = (sel * weight).astype(BF)
        return carry

    def project(w, part, shift):
        where = cols(net.dx(shift))
        tile = 320

        def body(i, carry):
            at = pl.ds(pl.multiple_of(i * tile, tile), tile)
            part[at, where] = lax.dot_general(
                rows[at, :], w[where, :], (((1,), (1,)), ((), ())), preferred_element_type=F32
            ).astype(BF)
            return carry

        lax.fori_loop(0, ROWS // tile, body, 0)

    def flow(w, part, out, bufs):
        project(w, part, 2)
        red = reduce_flow(net, part, out, *bufs)
        next(red)
        project(w, part, 1)
        project(w, part, -1)
        next(red)
        project(w, part, 0)
        yield
        yield from red

    bufs_a = [r.at[0] for r in (hop_r, hop_l, in_r, in_l, y_out, y_in)]
    bufs_b = [r.at[1] for r in (hop_r, hop_l, in_r, in_l, y_out, y_in)]
    def act_hidden(i, carry):
        at = pl.ds(pl.multiple_of(i * 160, 160), 160)
        pre = acc_a[at, :]
        hid_s[at, :] = (pre * jax.nn.sigmoid(pre)).astype(BF)
        return carry

    def act_slope(i, carry):
        at = pl.ds(pl.multiple_of(i * 160, 160), 160)
        pre, back = acc_a[at, :], acc_b[at, :]
        sig = jax.nn.sigmoid(pre)
        slope_o[at, :] = (back * sig * (1.0 + pre * (1.0 - sig))).astype(BF)
        return carry

    def pre_path():
        lax.fori_loop(0, 16, pick_tok, 0)
        yield from flow(wg, part_a, acc_a, bufs_a)
        lax.fori_loop(0, ROWS // 160, act_hidden, 0)
        yield from together(
            whole_flow(net, hid_s, hidden, local_sem.at[1]),
            move_flow(net, hid_s, old, new, spread, picked, hid_moved, local_sem.at[2]),
        )

    def back_path():
        yield from cots
        lax.fori_loop(0, 16, pick_cot, 0)
        yield from flow(wd, part_b, acc_b, bufs_b)

    run_together(pre_path(), back_path())
    lax.fori_loop(0, ROWS // 160, act_slope, 0)
    net.drain()


def dispatch(*args):
    width = args[0].shape[1]
    vm = pl.BlockSpec(memory_space=pltpu.VMEM)
    sm = pl.BlockSpec(memory_space=pltpu.SMEM)
    sds = jax.ShapeDtypeStruct
    half = ROWS // 2
    return pl.pallas_call(
        dispatch_kernel,
        out_shape=(
            sds((ROWS, 128), BF),
            sds((ROWS, 1024), BF),
            sds((ROWS, 128), BF),
            sds((ROWS, width), BF),
            sds((ROWS, width), BF),
            sds((16, 256), F32),
            sds((16, 256), F32),
        ),
        in_specs=[vm] * 5 + [sm] * 2,
        out_specs=(vm,) * 7,
        scratch_shapes=[
            pltpu.VMEM((16, 2, TOK, width), BF),
            pltpu.VMEM((16, 2, TOK, width), BF),
            pltpu.VMEM((2, 16, 16, 128), F32),
            pltpu.VMEM((ROWS, width), BF),
            pltpu.VMEM((ROWS, 1024), BF),
            pltpu.VMEM((ROWS, 1024), BF),
            pltpu.VMEM((ROWS, 128), F32),
            pltpu.VMEM((ROWS, 128), F32),
            pltpu.VMEM((2, half, 256), BF),
            pltpu.VMEM((2, half, 256), BF),
            pltpu.VMEM((2, ROWS, 256), BF),
            pltpu.VMEM((2, ROWS, 256), BF),
            pltpu.VMEM((2, ROWS, 128), BF),
            pltpu.VMEM((2, ROWS, 128), BF),
            pltpu.VMEM((16, 256), F32),
            pltpu.VMEM((16, 256), F32),
            pltpu.VMEM((ROWS, 128), BF),
            pltpu.VMEM((NZ, 4, ROWS // NZ, 128), BF),
            pltpu.VMEM((NZ, ROWS // NZ, 128), BF),
            pltpu.SemaphoreType.DMA((3,)),
            pltpu.SemaphoreType.DMA((256,)),
            pltpu.SemaphoreType.DMA((256,)),
        ],
        compiler_params=pltpu.CompilerParams(
            collective_id=0, has_side_effects=True, vmem_limit_bytes=VMEM_LIMIT
        ),
    )(*args)


def add_into(dst, *srcs):
    lead, rows = dst.shape[:-2], dst.shape[-2]

    def body(i, carry):
        at = pl.ds(pl.multiple_of(i * 16, 16), 16)
        for j in range(lead[0] if lead else 1):
            where = (j, at) if lead else (at,)
            acc = dst[where].astype(F32)
            for src in srcs:
                acc = acc + src[where].astype(F32)
            dst[where] = acc.astype(BF)
        return carry

    lax.fori_loop(0, rows // 16, body, 0)


def return_flow(net, contribution, to_core, from_core, sums, y_b, ring_ra, ring_la, ring_rb, ring_lb, y_a, out):
    z, h, c = net.z, net.h, net.c
    width = out.shape[-1]
    other_y, other_c = net.at(h=1 - h), net.at(c=1 - c)
    right, left = net.at(z=net.dz(1)), net.at(z=net.dz(-1))
    ra, rb = pl.ds(0, HALF), pl.ds(HALF, HALF)
    a_first, a_last = pl.ds(0, QUART), pl.ds(QUART, QUART)
    b_first, b_last = pl.ds(HALF, QUART), pl.ds(HALF + QUART, QUART)
    both = slice(None)
    core, yb = {}, {}

    def give(s):
        for k in ((4,), (3, -3), (2, -2), (1, -1), (0,), ())[s]:
            zt = net.dz(k)
            to_core[zt] = contribution((1 - c) * NZ + zt).astype(BF).reshape(2, TOK, width)
            core[k] = net.send(to_core.at[zt], from_core.at[zt], other_c)

    give(0)
    yield
    ar = al = br = bl = None
    for s in range(5):
        ks = (4,) if s == 0 else (0,) if s == 4 else (4 - s, s - 4)
        give(s + 1)
        for k in ks:
            zt = net.dz(k)
            net.arrive(from_core.at[zt], core[k])
            got = from_core[zt].astype(F32).reshape(2 * TOK, width)
            sums[zt] = (contribution(c * NZ + zt) + got).astype(BF).reshape(2, TOK, width)
            yb[k] = net.send(sums.at[zt, 1 - h, rb], y_b.at[zt], other_y)
        zr, zl = net.dz(4 - s), net.dz(s - 4)
        if s == 0:
            ar = net.send(sums.at[zr, both, a_first], ring_ra.at[0, both, a_first], right)
            al = net.send(sums.at[zr, both, a_last], ring_la.at[0, both, a_last], left)
            net.arrive(y_b.at[zr], yb[4])
            add_into(sums.at[zr, h, rb], y_b.at[zr])
            br = net.send(sums.at[zr, h, b_first], ring_rb.at[0, a_first], right)
            bl = net.send(sums.at[zr, h, b_last], ring_lb.at[0, a_last], left)
            yield
            continue
        at_r, at_l = (a_first, a_last) if s == 1 else (ra, ra)
        bt_r, bt_l = (b_first, b_last) if s == 1 else (rb, rb)
        if s < 4:
            net.arrive(ring_ra.at[s - 1, both, at_r], ar)
            add_into(sums.at[zr, both, at_r], ring_ra.at[s - 1, both, at_r])
            ar = net.send(sums.at[zr, both, ra], ring_ra.at[s], right)
            net.arrive(ring_la.at[s - 1, both, at_l], al)
            add_into(sums.at[zl, both, at_l], ring_la.at[s - 1, both, at_l])
            al = net.send(sums.at[zl, both, ra], ring_la.at[s], left)
            for k in ks:
                net.arrive(y_b.at[net.dz(k)], yb[k])
                add_into(sums.at[net.dz(k), h, rb], y_b.at[net.dz(k)])
            net.arrive(ring_rb.at[s - 1, at_r], br)
            add_into(sums.at[zr, h, bt_r], ring_rb.at[s - 1, at_r])
            br = net.send(sums.at[zr, h, rb], ring_rb.at[s], right)
            net.arrive(ring_lb.at[s - 1, at_l], bl)
            add_into(sums.at[zl, h, bt_l], ring_lb.at[s - 1, at_l])
            bl = net.send(sums.at[zl, h, rb], ring_lb.at[s], left)
            yield
            continue
        net.arrive(ring_ra.at[3], ar)
        net.arrive(ring_la.at[3], al)
        add_into(sums.at[z, both, ra], ring_ra.at[3], ring_la.at[3])
        ya = net.send(sums.at[z, 1 - h, ra], y_a, other_y)
        net.arrive(y_b.at[z], yb[0])
        net.arrive(ring_rb.at[3], br)
        net.arrive(ring_lb.at[3], bl)
        out[rb, :] = (
            sums[z, h, rb, :].astype(F32)
            + y_b[z].astype(F32)
            + ring_rb[3].astype(F32)
            + ring_lb[3].astype(F32)
        ).astype(BF)
        yield
        net.arrive(y_a, ya)
        out[ra, :] = (sums[z, h, ra, :].astype(F32) + y_a[...].astype(F32)).astype(BF)
    yield


ORDER = "bmf" "bf" "bf" "mhbf" "hbf" "mhbf" "mhsbf" "hsbd" "sb" "sb" "sb" "bg"


def finish_kernel(
    slope_s, hidden, hid_moved, rows_new, cot_new, rank, weight, wg, wd, old, new,
    layer_out, token_grads, grad_gate, grad_down,
    slope, hidden_new, slope_new, spread, picked, moved, out_rows, back_rows,
    to_core, from_core, sums, y_b, ring_ra, ring_la, ring_rb, ring_lb, y_a,
    local_sem, send_sem, recv_sem,
):
    net = Links(send_sem, recv_sem)
    net.barrier()
    tile = 320

    def weighted(i, carry):
        at = pl.ds(pl.multiple_of(i * tile, tile), tile)
        w = jnp.concatenate(
            [
                jnp.sum(
                    picker(rank, i * 4 + j) * weight[pl.ds(i * 4 + j, 1), :], axis=1, keepdims=True
                )
                for j in range(4)
            ],
            axis=0,
        )
        out = jnp.dot(hidden[at, :], wd[...], preferred_element_type=F32)
        out_rows[at, :] = (out * w).astype(BF)
        return carry

    def plain(i, carry):
        at = pl.ds(pl.multiple_of(i * tile, tile), tile)
        back_rows[at, :] = jnp.dot(slope[at, :], wg[...], preferred_element_type=F32).astype(BF)
        return carry

    def placed(rows):
        def contribution(p):
            sel = picker(rank, p).astype(BF)
            at = pl.ds(pl.multiple_of(p * PAIR, 16), PAIR)
            return lax.dot_general(sel, rows[at, :], (((0,), (0,)), ((), ())), preferred_element_type=F32)

        return contribution

    def outer(left, right, out):
        def body(i, carry):
            at = pl.ds(pl.multiple_of(i * 256, 256), 256)
            out[at, :] = lax.dot_general(
                left[:, at], right[...], (((0,), (0,)), ((), ())), preferred_element_type=F32
            ).astype(BF)
            return carry

        lax.fori_loop(0, 4, body, 0)

    bufs = (to_core, from_core, sums, y_b, ring_ra, ring_la, ring_rb, ring_lb, y_a)

    def forward():
        lax.fori_loop(0, ROWS // tile, weighted, 0)
        yield from return_flow(net, placed(out_rows), *[b.at[0] for b in bufs], layer_out)

    def backward():
        yield from whole_flow(net, slope_s, slope, local_sem.at[0])
        lax.fori_loop(0, ROWS // tile, plain, 0)
        yield from return_flow(net, placed(back_rows), *[b.at[1] for b in bufs], token_grads)

    flows = {
        "b": backward(),
        "f": forward(),
        "m": move_flow(net, slope_s, old, new, spread, picked, moved, local_sem.at[1]),
        "h": whole_flow(net, hid_moved, hidden_new, local_sem.at[2]),
        "s": whole_flow(net, moved, slope_new, local_sem.at[3]),
    }
    for step in ORDER:
        if step == "d":
            outer(hidden_new, cot_new, grad_down)
        elif step == "g":
            outer(slope_new, rows_new, grad_gate)
        else:
            next(flows[step], None)
    net.drain()


def finish(*args):
    width = args[3].shape[1]
    vm = pl.BlockSpec(memory_space=pltpu.VMEM)
    sm = pl.BlockSpec(memory_space=pltpu.SMEM)
    sds = jax.ShapeDtypeStruct
    n = ROWS // NZ
    return pl.pallas_call(
        finish_kernel,
        out_shape=(
            sds((TOK, width), BF),
            sds((TOK, width), BF),
            sds((1024, width), BF),
            sds((1024, width), BF),
        ),
        in_specs=[vm] * 9 + [sm] * 2,
        out_specs=(vm,) * 4,
        scratch_shapes=[
            pltpu.VMEM((ROWS, 1024), BF),
            pltpu.VMEM((ROWS, 1024), BF),
            pltpu.VMEM((ROWS, 1024), BF),
            pltpu.VMEM((NZ, 4, n, 128), BF),
            pltpu.VMEM((NZ, n, 128), BF),
            pltpu.VMEM((ROWS, 128), BF),
            pltpu.VMEM((ROWS, width), BF),
            pltpu.VMEM((ROWS, width), BF),
            pltpu.VMEM((2, NZ, 2, TOK, width), BF),
            pltpu.VMEM((2, NZ, 2, TOK, width), BF),
            pltpu.VMEM((2, NZ, 2, TOK, width), BF),
            pltpu.VMEM((2, NZ, HALF, width), BF),
            pltpu.VMEM((2, 4, 2, HALF, width), BF),
            pltpu.VMEM((2, 4, 2, HALF, width), BF),
            pltpu.VMEM((2, 4, HALF, width), BF),
            pltpu.VMEM((2, 4, HALF, width), BF),
            pltpu.VMEM((2, HALF, width), BF),
            pltpu.SemaphoreType.DMA((4,)),
            pltpu.SemaphoreType.DMA((256,)),
            pltpu.SemaphoreType.DMA((256,)),
        ],
        compiler_params=pltpu.CompilerParams(
            collective_id=1, has_side_effects=True, vmem_limit_bytes=VMEM_LIMIT
        ),
    )(*args)


def per_device(tokens, cotangent, expert_ids, gate_weights, owner_old, owner_new, w_gate, w_down):
    info = jnp.concatenate([expert_ids.T.astype(F32), gate_weights.T], axis=0)
    gate_here, down_here = w_gate[0], w_down[0]
    slope_s, hidden, hid_moved, rows_new, cot_new, rank, weight = dispatch(
        tokens, cotangent, info, gate_here, down_here, owner_old, owner_new
    )
    layer_out, token_grads, grad_gate, grad_down = finish(
        slope_s, hidden, hid_moved, rows_new, cot_new, rank, weight, gate_here, down_here, owner_old, owner_new
    )
    return (layer_out, token_grads, grad_gate[None], grad_down[None])


def solution(mesh):
    return jax.shard_map(
        per_device,
        mesh=mesh,
        in_specs=(
            P("expert", "hid"),
            P("expert", "hid"),
            P("expert", None),
            P("expert", None),
            P(),
            P(),
            P("expert", None, "hid"),
            P("expert", None, "hid"),
        ),
        out_specs=(
            P("expert", "hid"),
            P("expert", "hid"),
            P("expert", None, "hid"),
            P("expert", None, "hid"),
        ),
        check_vma=False,
    )
```

```python
import functools

import jax
import jax.numpy as jnp
from jax import lax
from jax.experimental import pallas as pl
from jax.experimental.pallas import tpu as pltpu
from jax.sharding import PartitionSpec as P

MESH = pl.DeviceIdType.MESH
BF = jnp.bfloat16
F32 = jnp.float32
VMEM_LIMIT = 62 << 20
NZ, CAP, TOK, HALF, QUART = 8, 40, 128, 64, 32
ROWS, PAIR, CHUNK = 1280, 80, 640
NEAR = (0, -1, 1, -2, 2, -3, 3, 4)


def place():
    e, d = lax.axis_index("expert"), lax.axis_index("hid")
    return e // 4, (e // 2) % 2, e % 2, d // 4, d % 4


class Links:
    def __init__(self, send_sem, recv_sem):
        self.z, self.h, self.c, self.lo, self.x = place()
        self.send_sem, self.recv_sem, self.used, self.sent = send_sem, recv_sem, 0, []

    def at(self, z=None, h=None, c=None, lo=None, x=None):
        z = self.z if z is None else z
        h = self.h if h is None else h
        c = self.c if c is None else c
        lo = self.lo if lo is None else lo
        x = self.x if x is None else x
        return (z * 4 + h * 2 + c, lo * 4 + x)

    def dz(self, k):
        return (self.z + k + NZ) % NZ

    def dx(self, k):
        return (self.x + k + 4) % 4

    def barrier(self):
        peers = [self.at(z=self.dz(k)) for k in range(1, NZ)]
        peers += [
            self.at(h=1 - self.h),
            self.at(c=1 - self.c),
            self.at(x=self.dx(1)),
            self.at(x=self.dx(-1)),
            self.at(lo=1 - self.lo),
        ]
        sem = pltpu.get_barrier_semaphore()
        for peer in peers:
            pl.semaphore_signal(sem, inc=1, device_id=peer, device_id_type=MESH)
        pl.semaphore_wait(sem, len(peers))

    def new(self):
        self.used += 1
        return self.used - 1

    def send(self, src, dst, peer, sem=None):
        i = self.new()
        copy = pltpu.make_async_remote_copy(
            src_ref=src,
            dst_ref=dst,
            send_sem=self.send_sem.at[i],
            recv_sem=self.recv_sem.at[i if sem is None else sem],
            device_id=peer,
            device_id_type=MESH,
        )
        copy.start()
        self.sent.append(copy)
        return i

    def arrive(self, ref, i):
        pltpu.make_async_copy(ref, ref, self.recv_sem.at[i]).wait()

    def drain(self):
        for copy in self.sent:
            copy.wait_send()
        self.sent = []


def gather_flow(net, own, full, local_sem, core_sems):
    z, h, c = net.z, net.h, net.c
    other_y, other_c = net.at(h=1 - h), net.at(c=1 - c)
    right, left = net.at(z=net.dz(1)), net.at(z=net.dz(-1))
    me = c * NZ + z
    ra, rb = pl.ds(0, HALF), pl.ds(HALF, HALF)
    a_first, a_last = pl.ds(0, QUART), pl.ds(QUART, QUART)
    b_first, b_last = pl.ds(HALF, QUART), pl.ds(HALF + QUART, QUART)
    keep = pltpu.make_async_copy(own, full.at[me, h], local_sem)
    keep.start()
    ya = net.send(own.at[ra], full.at[me, h, ra], other_y)
    b_right = net.send(own.at[rb], full.at[me, h, rb], right)
    b_left = net.send(own.at[rb], full.at[me, h, rb], left)
    keep.wait()
    yb = [net.send(full.at[me, h, rb], full.at[me, h, rb], other_y)]

    def to_core(k, what):
        slot = c * NZ + net.dz(k)
        net.send(full.at[(slot,) + what], full.at[(slot,) + what], other_c, sem=core_sems[k % NZ])

    to_core(0, (h, slice(None)))
    both = slice(None)
    net.arrive(full.at[me, 1 - h, ra], ya)
    a_right = net.send(full.at[me, both, ra], full.at[me, both, ra], right)
    a_left = net.send(full.at[me, both, ra], full.at[me, both, ra], left)
    to_core(0, (1 - h, ra))
    yield
    pending = [(0, yb[0])]
    for k in range(4):
        zr, zl = c * NZ + net.dz(-1 - k), c * NZ + net.dz(1 + k)
        last, nxt_last = k == 3, k == 2
        br, bl = (b_first, b_last) if last else (rb, rb)
        net.arrive(full.at[zr, h, br], b_right)
        if not last:
            rows = b_first if nxt_last else rb
            b_right = net.send(full.at[zr, h, rows], full.at[zr, h, rows], right)
        net.arrive(full.at[zl, h, bl], b_left)
        if not last:
            rows = b_last if nxt_last else rb
            b_left = net.send(full.at[zl, h, rows], full.at[zl, h, rows], left)
        fresh = [(-1 - k, net.send(full.at[zr, h, rb], full.at[zr, h, rb], other_y))]
        to_core(-1 - k, (h, rb))
        if not last:
            fresh.append((1 + k, net.send(full.at[zl, h, rb], full.at[zl, h, rb], other_y)))
            to_core(1 + k, (h, rb))
        ar, al = (a_first, a_last) if last else (ra, ra)
        net.arrive(full.at[zr, both, ar], a_right)
        if not last:
            rows = a_first if nxt_last else ra
            a_right = net.send(full.at[zr, both, rows], full.at[zr, both, rows], right)
        net.arrive(full.at[zl, both, al], a_left)
        if not last:
            rows = a_last if nxt_last else ra
            a_left = net.send(full.at[zl, both, rows], full.at[zl, both, rows], left)
        to_core(-1 - k, (both, ra))
        if not last:
            to_core(1 + k, (both, ra))
        for d, sem in pending:
            slot = c * NZ + net.dz(d)
            net.arrive(full.at[slot, 1 - h, rb], sem)
            to_core(d, (1 - h, rb))
        pending = fresh
        yield
    for d, sem in pending:
        slot = c * NZ + net.dz(d)
        net.arrive(full.at[slot, 1 - h, rb], sem)
        to_core(d, (1 - h, rb))
    yield


def small_gather(net, own, full, local_sem):
    z, h, c = net.z, net.h, net.c
    right, left = net.at(z=net.dz(1)), net.at(z=net.dz(-1))
    me = c * NZ + z
    keep = pltpu.make_async_copy(own, full.at[h, me], local_sem)
    keep.start()
    y = net.send(own, full.at[h, me], net.at(h=1 - h))
    keep.wait()
    net.arrive(full.at[1 - h, me], y)
    r = net.send(full.at[:, me], full.at[:, me], right)
    l = net.send(full.at[:, me], full.at[:, me], left)
    yield
    for k in range(4):
        zr, zl = c * NZ + net.dz(-1 - k), c * NZ + net.dz(1 + k)
        net.arrive(full.at[:, zr], r)
        if k < 3:
            r = net.send(full.at[:, zr], full.at[:, zr], right)
            net.arrive(full.at[:, zl], l)
            if k < 2:
                l = net.send(full.at[:, zl], full.at[:, zl], left)
        yield
    mine, theirs = pl.ds(pl.multiple_of(c * NZ, NZ), NZ), pl.ds(pl.multiple_of((1 - c) * NZ, NZ), NZ)
    i = net.send(full.at[:, mine], full.at[:, mine], net.at(c=1 - c))
    net.arrive(full.at[:, theirs], i)
    yield


def cols(xt, lo=None):
    if lo is None:
        return pl.ds(pl.multiple_of(xt * 256, 256), 256)
    return pl.ds(pl.multiple_of(xt * 256 + lo * 128, 128), 128)


def reduce_flow(net, part, out, hop_r, hop_l, in_r, in_l, y_out, y_in, start):
    x, lo = net.x, net.lo
    right, left = net.at(x=net.dx(1)), net.at(x=net.dx(-1))
    n = CHUNK // 2
    r0, r1 = pl.ds(start, n), pl.ds(start + n, n)
    hop_r, hop_l = hop_r.at[pl.ds(start // 2, n)], hop_l.at[pl.ds(start // 2, n)]
    far, nr, nl, own = cols(net.dx(2)), cols(net.dx(1)), cols(net.dx(-1)), cols(x)
    s1 = net.send(part.at[r0, far], hop_r, right)
    s2 = net.send(part.at[r1, far], hop_l, left)
    yield
    s3 = net.send(part.at[r1, nr], in_r.at[r1], right)
    s4 = net.send(part.at[r0, nl], in_l.at[r0], left)
    yield
    tile = 160

    def add(dst_rows, where, src):
        def body(i, carry):
            at = pl.multiple_of(i * tile, tile)
            rows = pl.ds(pl.multiple_of(dst_rows + at, tile), tile)
            part[rows, where] = (
                part[rows, where].astype(F32) + src[pl.ds(at, tile), :].astype(F32)
            ).astype(BF)
            return carry

        lax.fori_loop(0, n // tile, body, 0)

    net.arrive(hop_r, s1)
    add(start, nr, hop_r)
    s5 = net.send(part.at[r0, nr], in_r.at[r0], right)
    net.arrive(hop_l, s2)
    add(start + n, nl, hop_l)
    s6 = net.send(part.at[r1, nl], in_l.at[r1], left)
    yield
    waits = {0: ((in_r, s5), (in_l, s4)), 1: ((in_r, s3), (in_l, s6))}
    ys = []
    for half in (1, 0):
        rows_half = (r0, r1)[half]
        for buf, sem in waits[half]:
            net.arrive(buf.at[rows_half], sem)

        def total(i, carry):
            rows = pl.ds(pl.multiple_of(start + half * n + i * tile, tile), tile)
            for side, keep in ((lo, True), (1 - lo, False)):
                inner = pl.ds(pl.multiple_of(side * 128, 128), 128)
                acc = (
                    part[rows, cols(x, side)].astype(F32)
                    + in_r[rows, inner].astype(F32)
                    + in_l[rows, inner].astype(F32)
                )
                if keep:
                    out[rows, :] = acc
                else:
                    y_out[rows, :] = acc.astype(BF)
            return carry

        lax.fori_loop(0, n // tile, total, 0)
        ys.append((half, net.send(y_out.at[rows_half], y_in.at[rows_half], net.at(lo=1 - lo))))
    yield
    for half, sem in ys:
        net.arrive(y_in.at[(r0, r1)[half]], sem)

        def last(i, carry):
            rows = pl.ds(pl.multiple_of(start + half * n + i * tile, tile), tile)
            out[rows, :] = out[rows, :] + y_in[rows, :].astype(F32)
            return carry

        lax.fori_loop(0, n // tile, last, 0)


def together(*flows):
    flows = list(flows)
    while flows:
        for flow in list(flows):
            try:
                next(flow)
            except StopIteration:
                flows.remove(flow)
        yield


def run_together(*flows):
    for _ in together(*flows):
        pass


def later(turns, flow):
    for _ in range(turns):
        yield
    yield from flow


def whole_flow(net, own, full, local_sem):
    x, lo = net.x, net.lo
    n = ROWS // 2
    right, left, other = net.at(x=net.dx(1)), net.at(x=net.dx(-1)), net.at(lo=1 - lo)
    h0, h1, rows = pl.ds(0, n), pl.ds(n, n), (pl.ds(0, n), pl.ds(n, n))
    mine = cols(x, lo)
    keep = pltpu.make_async_copy(own, full.at[:, mine], local_sem)
    keep.start()
    ys = [net.send(own.at[r], full.at[r, mine], other) for r in rows]
    keep.wait()
    yield

    def fwd(r, where, peer):
        return net.send(full.at[r, where], full.at[r, where], peer)

    one_r, one_l = [], []
    for r, y in zip(rows, ys):
        net.arrive(full.at[r, cols(x, 1 - lo)], y)
        one_r.append(fwd(r, cols(x), right))
        one_l.append(fwd(r, cols(x), left))
    yield
    xl, xr, xf = net.dx(-1), net.dx(1), net.dx(2)
    net.arrive(full.at[h0, cols(xl)], one_r[0])
    two_r = fwd(h0, cols(xl), right)
    net.arrive(full.at[h0, cols(xr)], one_l[0])
    yield
    net.arrive(full.at[h1, cols(xr)], one_l[1])
    two_l = fwd(h1, cols(xr), left)
    net.arrive(full.at[h1, cols(xl)], one_r[1])
    yield
    net.arrive(full.at[h0, cols(xf)], two_r)
    net.arrive(full.at[h1, cols(xf)], two_l)
    yield


def look_up(table, wanted, value):
    found = jnp.int32(0)
    for i in range(32):
        found = found + jnp.where(table[i] == wanted, value(i), 0)
    return found


def move_flow(net, shard, old, new, spread, picked, moved, local_sem):
    z, h, c = net.z, net.h, net.c
    n = ROWS // NZ
    hc, yc = h * 2 + c, (1 - h) * 2 + c
    far_first = (4, 3, -3, 2, -2, 1, -1)

    def eighth(zt):
        return pl.ds(pl.multiple_of(zt * n, n), n)

    keep = pltpu.make_async_copy(shard.at[eighth(z)], spread.at[z, hc], local_sem)
    keep.start()
    sems = []
    for k in far_first:
        zt = net.dz(k)
        sems.append((-k, net.send(shard.at[eighth(zt)], spread.at[z, hc], net.at(z=zt))))
    keep.wait()
    yield
    for k, sem in sems:
        net.arrive(spread.at[net.dz(k), hc], sem)
    s = net.send(spread.at[:, hc], spread.at[:, hc], net.at(h=1 - h))
    t = net.send(spread.at[:, hc], spread.at[:, hc], net.at(c=1 - c))
    yield
    net.arrive(spread.at[:, yc], s)
    u = net.send(spread.at[:, yc], spread.at[:, yc], net.at(c=1 - c))
    net.arrive(spread.at[:, h * 2 + 1 - c], t)
    net.arrive(spread.at[:, (1 - h) * 2 + 1 - c], u)

    def pick(i, carry):
        source = look_up(new, i * 4 + hc, lambda e: old[e])
        picked[i] = spread[source // 4, source % 4]
        return carry

    lax.fori_loop(0, NZ, pick, 0)
    keep = pltpu.make_async_copy(picked.at[z], moved.at[eighth(z)], local_sem)
    keep.start()
    sems = []
    for k in far_first:
        zt = net.dz(k)
        sems.append((-k, net.send(picked.at[zt], moved.at[eighth(z)], net.at(z=zt))))
    keep.wait()
    yield
    for k, sem in sems:
        net.arrive(moved.at[eighth(net.dz(k))], sem)
    yield


def ranks(info, expert, rank_ref, weight_ref):
    expert = expert.astype(F32)
    row = lax.broadcasted_iota(jnp.int32, (TOK, TOK), 0)
    tri = jnp.where(row < lax.broadcasted_iota(jnp.int32, (TOK, TOK), 1), 1.0, 0.0).astype(BF)
    for side in range(2):
        hit = info[side, :, 0:8, :] == expert
        mask = jnp.max(jnp.where(hit, 1.0, 0.0), axis=1)
        weight = jnp.sum(jnp.where(hit, info[side, :, 8:16, :], 0.0), axis=1)
        before = jnp.dot(mask.astype(BF), tri, preferred_element_type=F32)
        where = pl.ds(side * TOK, TOK)
        rank_ref[:, where] = jnp.where(mask > 0.5, before + float(side * CAP), -1.0)
        weight_ref[:, where] = weight


def picker(rank_ref, p):
    slots = lax.broadcasted_iota(jnp.int32, (PAIR, 2 * TOK), 0).astype(F32)
    return jnp.where(slots == rank_ref[pl.ds(p, 1), :], 1.0, 0.0)


FIRST = "it" "it" "itk" "ikt" "ikir" "p" "tpkt" "qpu" "pq" "k" "qqhwm" "ku" "w" "v" "um" "w" "v" "u" "mw" "v" "w" "vm"


def dispatch_kernel(
    tok, cot, info, wg_in, wd_in, old, new,
    slope_o, hidden_o, hid_moved, rows_new_o, cot_new_o, rank_old, weight_old,
    wg, wd, hidden, rows_new, cot_new, tok_all, cot_all, info_all, rows, rows_b, part_a, part_b, acc_a, acc_b,
    hop_r, hop_l, in_r, in_l, y_out, y_in,
    rank_new, weight_new, hid_s, spread, picked,
    local_sem, send_sem, recv_sem,
):
    net = Links(send_sem, recv_sem)
    load_g = pltpu.make_async_copy(wg_in, wg, local_sem.at[3])
    load_d = pltpu.make_async_copy(wd_in, wd, local_sem.at[4])
    keep_rows = pltpu.make_async_copy(rows_new, rows_new_o, local_sem.at[5])
    keep_cot = pltpu.make_async_copy(cot_new, cot_new_o, local_sem.at[6])
    keep_hidden = pltpu.make_async_copy(hidden, hidden_o, local_sem.at[7])
    load_g.start()
    load_d.start()
    net.barrier()
    tok_sems = [net.new() for _ in range(NZ)]
    cot_sems = [net.new() for _ in range(NZ)]
    bufs_a = [r.at[0] for r in (hop_r, hop_l, in_r, in_l, y_out, y_in)]
    bufs_b = [r.at[1] for r in (hop_r, hop_l, in_r, in_l, y_out, y_in)]

    def slabs(chunk):
        return NEAR[:4] if chunk == 0 else NEAR[4:]

    def landed(full, sems, chunk):
        for k in slabs(chunk):
            net.arrive(full.at[(1 - net.c) * NZ + net.dz(k)], sems[k % NZ])

    def pairs(chunk):
        for i, k in enumerate(slabs(chunk)):
            for side in range(2):
                yield (chunk * 8 + i * 2 + side) * PAIR, side * NZ + net.dz(k)

    def pick_tok(chunk):
        for near, p in pairs(chunk):
            block = tok_all[p].reshape(2 * TOK, tok_all.shape[-1])
            at = pl.ds(pl.multiple_of(p * PAIR, 16), PAIR)
            sel = picker(rank_old, p).astype(BF)
            rows[pl.ds(near, PAIR), :] = jnp.dot(sel, block, preferred_element_type=F32).astype(BF)
            sel = picker(rank_new, p).astype(BF)
            rows_new[at, :] = jnp.dot(sel, block, preferred_element_type=F32).astype(BF)

    def pick_cot(chunk):
        for near, p in pairs(chunk):
            block = cot_all[p].reshape(2 * TOK, cot_all.shape[-1])
            at = pl.ds(pl.multiple_of(p * PAIR, 16), PAIR)
            for rank_ref, weight_ref, out, where in (
                (rank_old, weight_old, rows_b, pl.ds(near, PAIR)),
                (rank_new, weight_new, cot_new, at),
            ):
                hit = picker(rank_ref, p)
                weight = jnp.sum(hit * weight_ref[pl.ds(p, 1), :], axis=1, keepdims=True)
                sel = jnp.dot(hit.astype(BF), block, preferred_element_type=F32)
                out[where, :] = (sel * weight).astype(BF)

    def project(source, w, part, shift, chunk):
        where = cols(net.dx(shift))
        tile = 320

        def body(i, carry):
            at = pl.ds(pl.multiple_of(chunk * CHUNK + i * tile, tile), tile)
            part[at, where] = lax.dot_general(
                source[at, :], w[where, :], (((1,), (1,)), ((), ())), preferred_element_type=F32
            ).astype(BF)
            return carry

        lax.fori_loop(0, CHUNK // tile, body, 0)

    def flow(full, sems, pick, source, w, part, out, bufs, load, keep, chunk):
        landed(full, sems, chunk)
        pick(chunk)
        if chunk == 0:
            load.wait()
        else:
            keep.start()
        project(source, w, part, 2, chunk)
        red = reduce_flow(net, part, out, *bufs, chunk * CHUNK)
        next(red)
        project(source, w, part, 1, chunk)
        project(source, w, part, -1, chunk)
        next(red)
        project(source, w, part, 0, chunk)
        yield
        yield from red

    def spread_rows(out, value):
        for chunk in range(2):
            for near, p in pairs(chunk):
                out[pl.ds(pl.multiple_of(p * PAIR, 16), PAIR), :] = value(pl.ds(near, PAIR)).astype(BF)

    def act_hidden(at):
        pre = acc_a[at, :]
        return pre * jax.nn.sigmoid(pre)

    def act_slope(at):
        pre, back = acc_a[at, :], acc_b[at, :]
        sig = jax.nn.sigmoid(pre)
        return back * sig * (1.0 + pre * (1.0 - sig))

    flows = {
        "i": small_gather(net, info, info_all, local_sem.at[0]),
        "t": gather_flow(net, tok, tok_all, local_sem.at[1], tok_sems),
        "k": gather_flow(net, cot, cot_all, local_sem.at[2], cot_sems),
        "w": whole_flow(net, hid_s, hidden, local_sem.at[1]),
        "m": move_flow(net, hid_s, old, new, spread, picked, hid_moved, local_sem.at[2]),
    }
    for name, chunk in (("p", 0), ("q", 1)):
        flows[name] = flow(tok_all, tok_sems, pick_tok, rows, wg, part_a, acc_a, bufs_a, load_g, keep_rows, chunk)
    for name, chunk in (("u", 0), ("v", 1)):
        flows[name] = flow(cot_all, cot_sems, pick_cot, rows_b, wd, part_b, acc_b, bufs_b, load_d, keep_cot, chunk)
    me = net.z * 4 + net.h * 2 + net.c
    for step in FIRST:
        if step == "r":
            ranks(info_all, look_up(old, me, jnp.int32), rank_old, weight_old)
            ranks(info_all, look_up(new, me, jnp.int32), rank_new, weight_new)
        elif step == "h":
            spread_rows(hid_s, act_hidden)
        else:
            next(flows[step], None)
    keep_hidden.start()
    spread_rows(slope_o, act_slope)
    keep_rows.wait()
    keep_cot.wait()
    keep_hidden.wait()
    net.drain()


def dispatch(*args):
    width = args[0].shape[1]
    vm = pl.BlockSpec(memory_space=pltpu.VMEM)
    sm = pl.BlockSpec(memory_space=pltpu.SMEM)
    hbm = pl.BlockSpec(memory_space=pl.ANY)
    sds = jax.ShapeDtypeStruct
    half = ROWS // 2
    return pl.pallas_call(
        dispatch_kernel,
        out_shape=(
            sds((ROWS, 128), BF),
            sds((ROWS, 1024), BF),
            sds((ROWS, 128), BF),
            sds((ROWS, width), BF),
            sds((ROWS, width), BF),
            sds((16, 256), F32),
            sds((16, 256), F32),
        ),
        in_specs=[vm] * 3 + [hbm] * 2 + [sm] * 2,
        out_specs=(vm, hbm, vm, hbm, hbm, vm, vm),
        scratch_shapes=[
            pltpu.VMEM((1024, width), BF),
            pltpu.VMEM((1024, width), BF),
            pltpu.VMEM((ROWS, 1024), BF),
            pltpu.VMEM((ROWS, width), BF),
            pltpu.VMEM((ROWS, width), BF),
            pltpu.VMEM((16, 2, TOK, width), BF),
            pltpu.VMEM((16, 2, TOK, width), BF),
            pltpu.VMEM((2, 16, 16, 128), F32),
            pltpu.VMEM((ROWS, width), BF),
            pltpu.VMEM((ROWS, width), BF),
            pltpu.VMEM((ROWS, 1024), BF),
            pltpu.VMEM((ROWS, 1024), BF),
            pltpu.VMEM((ROWS, 128), F32),
            pltpu.VMEM((ROWS, 128), F32),
            pltpu.VMEM((2, half, 256), BF),
            pltpu.VMEM((2, half, 256), BF),
            pltpu.VMEM((2, ROWS, 256), BF),
            pltpu.VMEM((2, ROWS, 256), BF),
            pltpu.VMEM((2, ROWS, 128), BF),
            pltpu.VMEM((2, ROWS, 128), BF),
            pltpu.VMEM((16, 256), F32),
            pltpu.VMEM((16, 256), F32),
            pltpu.VMEM((ROWS, 128), BF),
            pltpu.VMEM((NZ, 4, ROWS // NZ, 128), BF),
            pltpu.VMEM((NZ, ROWS // NZ, 128), BF),
            pltpu.SemaphoreType.DMA((8,)),
            pltpu.SemaphoreType.DMA((256,)),
            pltpu.SemaphoreType.DMA((256,)),
        ],
        compiler_params=pltpu.CompilerParams(
            collective_id=0, has_side_effects=True, vmem_limit_bytes=VMEM_LIMIT
        ),
    )(*args)


def add_into(dst, *srcs):
    lead, rows = dst.shape[:-2], dst.shape[-2]

    def body(i, carry):
        at = pl.ds(pl.multiple_of(i * 16, 16), 16)
        for j in range(lead[0] if lead else 1):
            where = (j, at) if lead else (at,)
            acc = dst[where].astype(F32)
            for src in srcs:
                acc = acc + src[where].astype(F32)
            dst[where] = acc.astype(BF)
        return carry

    lax.fori_loop(0, rows // 16, body, 0)


def return_flow(net, contribution, to_core, from_core, sums, y_b, ring_ra, ring_la, ring_rb, ring_lb, y_a, out):
    z, h, c = net.z, net.h, net.c
    width = out.shape[-1]
    other_y, other_c = net.at(h=1 - h), net.at(c=1 - c)
    right, left = net.at(z=net.dz(1)), net.at(z=net.dz(-1))
    ra, rb = pl.ds(0, HALF), pl.ds(HALF, HALF)
    a_first, a_last = pl.ds(0, QUART), pl.ds(QUART, QUART)
    b_first, b_last = pl.ds(HALF, QUART), pl.ds(HALF + QUART, QUART)
    both = slice(None)
    core, yb = {}, {}

    def give(s):
        for k in ((4,), (3, -3), (2, -2), (1, -1), (0,), ())[s]:
            zt = net.dz(k)
            to_core[zt] = contribution((1 - c) * NZ + zt).astype(BF).reshape(2, TOK, width)
            core[k] = net.send(to_core.at[zt], from_core.at[zt], other_c)

    give(0)
    yield
    ar = al = br = bl = None
    for s in range(5):
        ks = (4,) if s == 0 else (0,) if s == 4 else (4 - s, s - 4)
        give(s + 1)
        for k in ks:
            zt = net.dz(k)
            net.arrive(from_core.at[zt], core[k])
            got = from_core[zt].astype(F32).reshape(2 * TOK, width)
            sums[zt] = (contribution(c * NZ + zt) + got).astype(BF).reshape(2, TOK, width)
            yb[k] = net.send(sums.at[zt, 1 - h, rb], y_b.at[zt], other_y)
        zr, zl = net.dz(4 - s), net.dz(s - 4)
        if s == 0:
            ar = net.send(sums.at[zr, both, a_first], ring_ra.at[0, both, a_first], right)
            al = net.send(sums.at[zr, both, a_last], ring_la.at[0, both, a_last], left)
            net.arrive(y_b.at[zr], yb[4])
            add_into(sums.at[zr, h, rb], y_b.at[zr])
            br = net.send(sums.at[zr, h, b_first], ring_rb.at[0, a_first], right)
            bl = net.send(sums.at[zr, h, b_last], ring_lb.at[0, a_last], left)
            yield
            continue
        at_r, at_l = (a_first, a_last) if s == 1 else (ra, ra)
        bt_r, bt_l = (b_first, b_last) if s == 1 else (rb, rb)
        if s < 4:
            net.arrive(ring_ra.at[s - 1, both, at_r], ar)
            add_into(sums.at[zr, both, at_r], ring_ra.at[s - 1, both, at_r])
            ar = net.send(sums.at[zr, both, ra], ring_ra.at[s], right)
            net.arrive(ring_la.at[s - 1, both, at_l], al)
            add_into(sums.at[zl, both, at_l], ring_la.at[s - 1, both, at_l])
            al = net.send(sums.at[zl, both, ra], ring_la.at[s], left)
            for k in ks:
                net.arrive(y_b.at[net.dz(k)], yb[k])
                add_into(sums.at[net.dz(k), h, rb], y_b.at[net.dz(k)])
            net.arrive(ring_rb.at[s - 1, at_r], br)
            add_into(sums.at[zr, h, bt_r], ring_rb.at[s - 1, at_r])
            br = net.send(sums.at[zr, h, rb], ring_rb.at[s], right)
            net.arrive(ring_lb.at[s - 1, at_l], bl)
            add_into(sums.at[zl, h, bt_l], ring_lb.at[s - 1, at_l])
            bl = net.send(sums.at[zl, h, rb], ring_lb.at[s], left)
            yield
            continue
        net.arrive(ring_ra.at[3], ar)
        net.arrive(ring_la.at[3], al)
        add_into(sums.at[z, both, ra], ring_ra.at[3], ring_la.at[3])
        ya = net.send(sums.at[z, 1 - h, ra], y_a, other_y)
        net.arrive(y_b.at[z], yb[0])
        net.arrive(ring_rb.at[3], br)
        net.arrive(ring_lb.at[3], bl)
        out[rb, :] = (
            sums[z, h, rb, :].astype(F32)
            + y_b[z].astype(F32)
            + ring_rb[3].astype(F32)
            + ring_lb[3].astype(F32)
        ).astype(BF)
        yield
        net.arrive(y_a, ya)
        out[ra, :] = (sums[z, h, ra, :].astype(F32) + y_a[...].astype(F32)).astype(BF)
    yield


ORDER = "bmf" "bf" "bf" "mhbf" "hbf" "mhbf" "mhsbf" "hsbd" "sb" "sb" "sb" "bg"


def finish_kernel(
    slope_s, hidden, hid_moved, rows_in, cot_in, rank, weight, wg_in, wd_in, old, new,
    layer_out, token_grads, grad_gate, grad_down,
    rows_new, cot_new, wg, wd,
    slope, hidden_new, slope_new, spread, picked, moved, out_rows, back_rows,
    to_core, from_core, sums, y_b, ring_ra, ring_la, ring_rb, ring_lb, y_a,
    local_sem, send_sem, recv_sem,
):
    net = Links(send_sem, recv_sem)
    loads = [
        pltpu.make_async_copy(src, dst, local_sem.at[4 + i])
        for i, (src, dst) in enumerate(((wd_in, wd), (wg_in, wg), (cot_in, cot_new), (rows_in, rows_new)))
    ]
    for load in loads:
        load.start()
    net.barrier()
    tile = 320

    def weighted(i, carry):
        at = pl.ds(pl.multiple_of(i * tile, tile), tile)
        w = jnp.concatenate(
            [
                jnp.sum(
                    picker(rank, i * 4 + j) * weight[pl.ds(i * 4 + j, 1), :], axis=1, keepdims=True
                )
                for j in range(4)
            ],
            axis=0,
        )
        out = jnp.dot(hidden[at, :], wd[...], preferred_element_type=F32)
        out_rows[at, :] = (out * w).astype(BF)
        return carry

    def plain(i, carry):
        at = pl.ds(pl.multiple_of(i * tile, tile), tile)
        back_rows[at, :] = jnp.dot(slope[at, :], wg[...], preferred_element_type=F32).astype(BF)
        return carry

    def placed(rows):
        def contribution(p):
            sel = picker(rank, p).astype(BF)
            at = pl.ds(pl.multiple_of(p * PAIR, 16), PAIR)
            return lax.dot_general(sel, rows[at, :], (((0,), (0,)), ((), ())), preferred_element_type=F32)

        return contribution

    def outer(left, right, out):
        def body(i, carry):
            at = pl.ds(pl.multiple_of(i * 256, 256), 256)
            out[at, :] = lax.dot_general(
                left[:, at], right[...], (((0,), (0,)), ((), ())), preferred_element_type=F32
            ).astype(BF)
            return carry

        lax.fori_loop(0, 4, body, 0)

    bufs = (to_core, from_core, sums, y_b, ring_ra, ring_la, ring_rb, ring_lb, y_a)

    def forward():
        loads[0].wait()
        lax.fori_loop(0, ROWS // tile, weighted, 0)
        yield from return_flow(net, placed(out_rows), *[b.at[0] for b in bufs], layer_out)

    def backward():
        yield from whole_flow(net, slope_s, slope, local_sem.at[0])
        loads[1].wait()
        lax.fori_loop(0, ROWS // tile, plain, 0)
        yield from return_flow(net, placed(back_rows), *[b.at[1] for b in bufs], token_grads)

    flows = {
        "b": backward(),
        "f": forward(),
        "m": move_flow(net, slope_s, old, new, spread, picked, moved, local_sem.at[1]),
        "h": whole_flow(net, hid_moved, hidden_new, local_sem.at[2]),
        "s": whole_flow(net, moved, slope_new, local_sem.at[3]),
    }
    for step in ORDER:
        if step == "d":
            loads[2].wait()
            outer(hidden_new, cot_new, grad_down)
        elif step == "g":
            loads[3].wait()
            outer(slope_new, rows_new, grad_gate)
        else:
            next(flows[step], None)
    net.drain()


def finish(*args):
    width = args[3].shape[1]
    vm = pl.BlockSpec(memory_space=pltpu.VMEM)
    sm = pl.BlockSpec(memory_space=pltpu.SMEM)
    hbm = pl.BlockSpec(memory_space=pl.ANY)
    sds = jax.ShapeDtypeStruct
    n = ROWS // NZ
    return pl.pallas_call(
        finish_kernel,
        out_shape=(
            sds((TOK, width), BF),
            sds((TOK, width), BF),
            sds((1024, width), BF),
            sds((1024, width), BF),
        ),
        in_specs=[vm] * 3 + [hbm] * 2 + [vm] * 2 + [hbm] * 2 + [sm] * 2,
        out_specs=(vm,) * 4,
        scratch_shapes=[
            pltpu.VMEM((ROWS, width), BF),
            pltpu.VMEM((ROWS, width), BF),
            pltpu.VMEM((1024, width), BF),
            pltpu.VMEM((1024, width), BF),
            pltpu.VMEM((ROWS, 1024), BF),
            pltpu.VMEM((ROWS, 1024), BF),
            pltpu.VMEM((ROWS, 1024), BF),
            pltpu.VMEM((NZ, 4, n, 128), BF),
            pltpu.VMEM((NZ, n, 128), BF),
            pltpu.VMEM((ROWS, 128), BF),
            pltpu.VMEM((ROWS, width), BF),
            pltpu.VMEM((ROWS, width), BF),
            pltpu.VMEM((2, NZ, 2, TOK, width), BF),
            pltpu.VMEM((2, NZ, 2, TOK, width), BF),
            pltpu.VMEM((2, NZ, 2, TOK, width), BF),
            pltpu.VMEM((2, NZ, HALF, width), BF),
            pltpu.VMEM((2, 4, 2, HALF, width), BF),
            pltpu.VMEM((2, 4, 2, HALF, width), BF),
            pltpu.VMEM((2, 4, HALF, width), BF),
            pltpu.VMEM((2, 4, HALF, width), BF),
            pltpu.VMEM((2, HALF, width), BF),
            pltpu.SemaphoreType.DMA((8,)),
            pltpu.SemaphoreType.DMA((256,)),
            pltpu.SemaphoreType.DMA((256,)),
        ],
        compiler_params=pltpu.CompilerParams(
            collective_id=1, has_side_effects=True, vmem_limit_bytes=VMEM_LIMIT
        ),
    )(*args)


def per_device(tokens, cotangent, expert_ids, gate_weights, owner_old, owner_new, w_gate, w_down):
    info = jnp.concatenate([expert_ids.T.astype(F32), gate_weights.T], axis=0)
    gate_here, down_here = w_gate[0], w_down[0]
    slope_s, hidden, hid_moved, rows_new, cot_new, rank, weight = dispatch(
        tokens, cotangent, info, gate_here, down_here, owner_old, owner_new
    )
    layer_out, token_grads, grad_gate, grad_down = finish(
        slope_s, hidden, hid_moved, rows_new, cot_new, rank, weight, gate_here, down_here, owner_old, owner_new
    )
    return (layer_out, token_grads, grad_gate[None], grad_down[None])


def solution(mesh):
    return jax.shard_map(
        per_device,
        mesh=mesh,
        in_specs=(
            P("expert", "hid"),
            P("expert", "hid"),
            P("expert", None),
            P("expert", None),
            P(),
            P(),
            P("expert", None, "hid"),
            P("expert", None, "hid"),
        ),
        out_specs=(
            P("expert", "hid"),
            P("expert", "hid"),
            P("expert", None, "hid"),
            P("expert", None, "hid"),
        ),
        check_vma=False,
    )
```

```python
import functools

import jax
import jax.numpy as jnp
from jax import lax
from jax.experimental import pallas as pl
from jax.experimental.pallas import tpu as pltpu
from jax.sharding import PartitionSpec as P

MESH = pl.DeviceIdType.MESH
BF = jnp.bfloat16
F32 = jnp.float32
VMEM_LIMIT = 62 << 20
NZ, CAP, TOK, HALF, QUART = 8, 40, 128, 64, 32
ROWS, PAIR, CHUNK = 1280, 80, 640
NEAR = (0, -1, 1, -2, 2, -3, 3, 4)


def place():
    e, d = lax.axis_index("expert"), lax.axis_index("hid")
    return e // 4, (e // 2) % 2, e % 2, d // 4, d % 4


class Links:
    def __init__(self, send_sem, recv_sem):
        self.z, self.h, self.c, self.lo, self.x = place()
        self.send_sem, self.recv_sem, self.used, self.sent = send_sem, recv_sem, 0, []

    def at(self, z=None, h=None, c=None, lo=None, x=None):
        z = self.z if z is None else z
        h = self.h if h is None else h
        c = self.c if c is None else c
        lo = self.lo if lo is None else lo
        x = self.x if x is None else x
        return (z * 4 + h * 2 + c, lo * 4 + x)

    def dz(self, k):
        return (self.z + k + NZ) % NZ

    def dx(self, k):
        return (self.x + k + 4) % 4

    def barrier(self):
        peers = [self.at(z=self.dz(k)) for k in range(1, NZ)]
        peers += [
            self.at(h=1 - self.h),
            self.at(c=1 - self.c),
            self.at(x=self.dx(1)),
            self.at(x=self.dx(-1)),
            self.at(lo=1 - self.lo),
        ]
        sem = pltpu.get_barrier_semaphore()
        for peer in peers:
            pl.semaphore_signal(sem, inc=1, device_id=peer, device_id_type=MESH)
        pl.semaphore_wait(sem, len(peers))

    def new(self):
        self.used += 1
        return self.used - 1

    def send(self, src, dst, peer, sem=None):
        i = self.new()
        copy = pltpu.make_async_remote_copy(
            src_ref=src,
            dst_ref=dst,
            send_sem=self.send_sem.at[i],
            recv_sem=self.recv_sem.at[i if sem is None else sem],
            device_id=peer,
            device_id_type=MESH,
        )
        copy.start()
        self.sent.append(copy)
        return i

    def arrive(self, ref, i):
        pltpu.make_async_copy(ref, ref, self.recv_sem.at[i]).wait()

    def drain(self):
        for copy in self.sent:
            copy.wait_send()
        self.sent = []


def gather_flow(net, own, full, local_sem, core_sems):
    z, h, c = net.z, net.h, net.c
    other_y, other_c = net.at(h=1 - h), net.at(c=1 - c)
    right, left = net.at(z=net.dz(1)), net.at(z=net.dz(-1))
    me = c * NZ + z
    ra, rb = pl.ds(0, HALF), pl.ds(HALF, HALF)
    a_first, a_last = pl.ds(0, QUART), pl.ds(QUART, QUART)
    b_first, b_last = pl.ds(HALF, QUART), pl.ds(HALF + QUART, QUART)
    keep = pltpu.make_async_copy(own, full.at[me, h], local_sem)
    keep.start()
    ya = net.send(own.at[ra], full.at[me, h, ra], other_y)
    b_right = net.send(own.at[rb], full.at[me, h, rb], right)
    b_left = net.send(own.at[rb], full.at[me, h, rb], left)
    keep.wait()
    yb = [net.send(full.at[me, h, rb], full.at[me, h, rb], other_y)]

    def to_core(k, what):
        slot = c * NZ + net.dz(k)
        net.send(full.at[(slot,) + what], full.at[(slot,) + what], other_c, sem=core_sems[k % NZ])

    to_core(0, (h, slice(None)))
    both = slice(None)
    net.arrive(full.at[me, 1 - h, ra], ya)
    a_right = net.send(full.at[me, both, ra], full.at[me, both, ra], right)
    a_left = net.send(full.at[me, both, ra], full.at[me, both, ra], left)
    to_core(0, (1 - h, ra))
    yield
    pending = [(0, yb[0])]
    for k in range(4):
        zr, zl = c * NZ + net.dz(-1 - k), c * NZ + net.dz(1 + k)
        last, nxt_last = k == 3, k == 2
        br, bl = (b_first, b_last) if last else (rb, rb)
        net.arrive(full.at[zr, h, br], b_right)
        if not last:
            rows = b_first if nxt_last else rb
            b_right = net.send(full.at[zr, h, rows], full.at[zr, h, rows], right)
        net.arrive(full.at[zl, h, bl], b_left)
        if not last:
            rows = b_last if nxt_last else rb
            b_left = net.send(full.at[zl, h, rows], full.at[zl, h, rows], left)
        fresh = [(-1 - k, net.send(full.at[zr, h, rb], full.at[zr, h, rb], other_y))]
        to_core(-1 - k, (h, rb))
        if not last:
            fresh.append((1 + k, net.send(full.at[zl, h, rb], full.at[zl, h, rb], other_y)))
            to_core(1 + k, (h, rb))
        ar, al = (a_first, a_last) if last else (ra, ra)
        net.arrive(full.at[zr, both, ar], a_right)
        if not last:
            rows = a_first if nxt_last else ra
            a_right = net.send(full.at[zr, both, rows], full.at[zr, both, rows], right)
        net.arrive(full.at[zl, both, al], a_left)
        if not last:
            rows = a_last if nxt_last else ra
            a_left = net.send(full.at[zl, both, rows], full.at[zl, both, rows], left)
        to_core(-1 - k, (both, ra))
        if not last:
            to_core(1 + k, (both, ra))
        for d, sem in pending:
            slot = c * NZ + net.dz(d)
            net.arrive(full.at[slot, 1 - h, rb], sem)
            to_core(d, (1 - h, rb))
        pending = fresh
        yield
    for d, sem in pending:
        slot = c * NZ + net.dz(d)
        net.arrive(full.at[slot, 1 - h, rb], sem)
        to_core(d, (1 - h, rb))
    yield


def small_gather(net, own, full, local_sem):
    z, h, c = net.z, net.h, net.c
    right, left = net.at(z=net.dz(1)), net.at(z=net.dz(-1))
    me = c * NZ + z
    keep = pltpu.make_async_copy(own, full.at[h, me], local_sem)
    keep.start()
    y = net.send(own, full.at[h, me], net.at(h=1 - h))
    keep.wait()
    net.arrive(full.at[1 - h, me], y)
    r = net.send(full.at[:, me], full.at[:, me], right)
    l = net.send(full.at[:, me], full.at[:, me], left)
    yield
    for k in range(4):
        zr, zl = c * NZ + net.dz(-1 - k), c * NZ + net.dz(1 + k)
        net.arrive(full.at[:, zr], r)
        if k < 3:
            r = net.send(full.at[:, zr], full.at[:, zr], right)
            net.arrive(full.at[:, zl], l)
            if k < 2:
                l = net.send(full.at[:, zl], full.at[:, zl], left)
        yield
    mine, theirs = pl.ds(pl.multiple_of(c * NZ, NZ), NZ), pl.ds(pl.multiple_of((1 - c) * NZ, NZ), NZ)
    i = net.send(full.at[:, mine], full.at[:, mine], net.at(c=1 - c))
    net.arrive(full.at[:, theirs], i)
    yield


def cols(xt, lo=None):
    if lo is None:
        return pl.ds(pl.multiple_of(xt * 256, 256), 256)
    return pl.ds(pl.multiple_of(xt * 256 + lo * 128, 128), 128)


def reduce_flow(net, part, out, hop_r, hop_l, in_r, in_l, y_out, y_in, start):
    x, lo = net.x, net.lo
    right, left = net.at(x=net.dx(1)), net.at(x=net.dx(-1))
    n = CHUNK // 2
    r0, r1 = pl.ds(start, n), pl.ds(start + n, n)
    hop_r, hop_l = hop_r.at[pl.ds(start // 2, n)], hop_l.at[pl.ds(start // 2, n)]
    far, nr, nl, own = cols(net.dx(2)), cols(net.dx(1)), cols(net.dx(-1)), cols(x)
    s1 = net.send(part.at[r0, far], hop_r, right)
    s2 = net.send(part.at[r1, far], hop_l, left)
    yield
    s3 = net.send(part.at[r1, nr], in_r.at[r1], right)
    s4 = net.send(part.at[r0, nl], in_l.at[r0], left)
    yield
    tile = 160

    def add(dst_rows, where, src):
        def body(i, carry):
            at = pl.multiple_of(i * tile, tile)
            rows = pl.ds(pl.multiple_of(dst_rows + at, tile), tile)
            part[rows, where] = (
                part[rows, where].astype(F32) + src[pl.ds(at, tile), :].astype(F32)
            ).astype(BF)
            return carry

        lax.fori_loop(0, n // tile, body, 0)

    net.arrive(hop_r, s1)
    add(start, nr, hop_r)
    s5 = net.send(part.at[r0, nr], in_r.at[r0], right)
    net.arrive(hop_l, s2)
    add(start + n, nl, hop_l)
    s6 = net.send(part.at[r1, nl], in_l.at[r1], left)
    yield
    waits = {0: ((in_r, s5), (in_l, s4)), 1: ((in_r, s3), (in_l, s6))}
    ys = []
    for half in (1, 0):
        rows_half = (r0, r1)[half]
        for buf, sem in waits[half]:
            net.arrive(buf.at[rows_half], sem)

        def total(i, carry):
            rows = pl.ds(pl.multiple_of(start + half * n + i * tile, tile), tile)
            for side, keep in ((lo, True), (1 - lo, False)):
                inner = pl.ds(pl.multiple_of(side * 128, 128), 128)
                acc = (
                    part[rows, cols(x, side)].astype(F32)
                    + in_r[rows, inner].astype(F32)
                    + in_l[rows, inner].astype(F32)
                )
                if keep:
                    out[rows, :] = acc
                else:
                    y_out[rows, :] = acc.astype(BF)
            return carry

        lax.fori_loop(0, n // tile, total, 0)
        ys.append((half, net.send(y_out.at[rows_half], y_in.at[rows_half], net.at(lo=1 - lo))))
    yield
    for half, sem in ys:
        net.arrive(y_in.at[(r0, r1)[half]], sem)

        def last(i, carry):
            rows = pl.ds(pl.multiple_of(start + half * n + i * tile, tile), tile)
            out[rows, :] = out[rows, :] + y_in[rows, :].astype(F32)
            return carry

        lax.fori_loop(0, n // tile, last, 0)


def together(*flows):
    flows = list(flows)
    while flows:
        for flow in list(flows):
            try:
                next(flow)
            except StopIteration:
                flows.remove(flow)
        yield


def run_together(*flows):
    for _ in together(*flows):
        pass


def later(turns, flow):
    for _ in range(turns):
        yield
    yield from flow


def whole_flow(net, own, full, local_sem):
    x, lo = net.x, net.lo
    n = ROWS // 2
    right, left, other = net.at(x=net.dx(1)), net.at(x=net.dx(-1)), net.at(lo=1 - lo)
    h0, h1, rows = pl.ds(0, n), pl.ds(n, n), (pl.ds(0, n), pl.ds(n, n))
    mine = cols(x, lo)
    keep = pltpu.make_async_copy(own, full.at[:, mine], local_sem)
    keep.start()
    ys = [net.send(own.at[r], full.at[r, mine], other) for r in rows]
    keep.wait()
    yield

    def fwd(r, where, peer):
        return net.send(full.at[r, where], full.at[r, where], peer)

    one_r, one_l = [], []
    for r, y in zip(rows, ys):
        net.arrive(full.at[r, cols(x, 1 - lo)], y)
        one_r.append(fwd(r, cols(x), right))
        one_l.append(fwd(r, cols(x), left))
    yield
    xl, xr, xf = net.dx(-1), net.dx(1), net.dx(2)
    net.arrive(full.at[h0, cols(xl)], one_r[0])
    two_r = fwd(h0, cols(xl), right)
    net.arrive(full.at[h0, cols(xr)], one_l[0])
    yield
    net.arrive(full.at[h1, cols(xr)], one_l[1])
    two_l = fwd(h1, cols(xr), left)
    net.arrive(full.at[h1, cols(xl)], one_r[1])
    yield
    net.arrive(full.at[h0, cols(xf)], two_r)
    net.arrive(full.at[h1, cols(xf)], two_l)
    yield


def look_up(table, wanted, value):
    found = jnp.int32(0)
    for i in range(32):
        found = found + jnp.where(table[i] == wanted, value(i), 0)
    return found


def move_flow(net, shard, old, new, spread, picked, moved, local_sem):
    z, h, c = net.z, net.h, net.c
    n = ROWS // NZ
    hc, yc = h * 2 + c, (1 - h) * 2 + c
    far_first = (4, 3, -3, 2, -2, 1, -1)

    def eighth(zt):
        return pl.ds(pl.multiple_of(zt * n, n), n)

    keep = pltpu.make_async_copy(shard.at[eighth(z)], spread.at[z, hc], local_sem)
    keep.start()
    sems = []
    for k in far_first:
        zt = net.dz(k)
        sems.append((-k, net.send(shard.at[eighth(zt)], spread.at[z, hc], net.at(z=zt))))
    keep.wait()
    yield
    for k, sem in sems:
        net.arrive(spread.at[net.dz(k), hc], sem)
    s = net.send(spread.at[:, hc], spread.at[:, hc], net.at(h=1 - h))
    t = net.send(spread.at[:, hc], spread.at[:, hc], net.at(c=1 - c))
    yield
    net.arrive(spread.at[:, yc], s)
    u = net.send(spread.at[:, yc], spread.at[:, yc], net.at(c=1 - c))
    net.arrive(spread.at[:, h * 2 + 1 - c], t)
    net.arrive(spread.at[:, (1 - h) * 2 + 1 - c], u)

    def pick(i, carry):
        source = look_up(new, i * 4 + hc, lambda e: old[e])
        picked[i] = spread[source // 4, source % 4]
        return carry

    lax.fori_loop(0, NZ, pick, 0)
    keep = pltpu.make_async_copy(picked.at[z], moved.at[eighth(z)], local_sem)
    keep.start()
    sems = []
    for k in far_first:
        zt = net.dz(k)
        sems.append((-k, net.send(picked.at[zt], moved.at[eighth(z)], net.at(z=zt))))
    keep.wait()
    yield
    for k, sem in sems:
        net.arrive(moved.at[eighth(net.dz(k))], sem)
    yield


def ranks(info, expert, rank_ref, weight_ref):
    expert = expert.astype(F32)
    row = lax.broadcasted_iota(jnp.int32, (TOK, TOK), 0)
    tri = jnp.where(row < lax.broadcasted_iota(jnp.int32, (TOK, TOK), 1), 1.0, 0.0).astype(BF)
    for side in range(2):
        hit = info[side, :, 0:8, :] == expert
        mask = jnp.max(jnp.where(hit, 1.0, 0.0), axis=1)
        weight = jnp.sum(jnp.where(hit, info[side, :, 8:16, :], 0.0), axis=1)
        before = jnp.dot(mask.astype(BF), tri, preferred_element_type=F32)
        where = pl.ds(side * TOK, TOK)
        rank_ref[:, where] = jnp.where(mask > 0.5, before + float(side * CAP), -1.0)
        weight_ref[:, where] = weight


def picker(rank_ref, p):
    slots = lax.broadcasted_iota(jnp.int32, (PAIR, 2 * TOK), 0).astype(F32)
    return jnp.where(slots == rank_ref[pl.ds(p, 1), :], 1.0, 0.0)


FIRST = "it" "it" "itk" "ikt" "ikir" "p" "tpkt" "qpu" "pq" "k" "qqhwm" "ku" "w" "v" "um" "w" "v" "u" "mw" "v" "w" "vm"


def dispatch_kernel(
    tok, cot, info, wg_in, wd_in, old, new,
    slope_o, hidden_o, hid_moved, rows_new_o, cot_new_o, rank_old, weight_old,
    wg, wd, hidden, rows_new, cot_new, tok_all, cot_all, info_all, rows, rows_b, part_a, part_b, acc_a, acc_b,
    hop_r, hop_l, in_r, in_l, y_out, y_in,
    rank_new, weight_new, hid_s, spread, picked,
    local_sem, send_sem, recv_sem,
):
    net = Links(send_sem, recv_sem)
    load_g = pltpu.make_async_copy(wg_in, wg, local_sem.at[3])
    load_d = pltpu.make_async_copy(wd_in, wd, local_sem.at[4])
    keep_rows = pltpu.make_async_copy(rows_new, rows_new_o, local_sem.at[5])
    keep_cot = pltpu.make_async_copy(cot_new, cot_new_o, local_sem.at[6])
    keep_hidden = pltpu.make_async_copy(hidden, hidden_o, local_sem.at[7])
    load_g.start()
    load_d.start()
    net.barrier()
    tok_sems = [net.new() for _ in range(NZ)]
    cot_sems = [net.new() for _ in range(NZ)]
    bufs_a = [r.at[0] for r in (hop_r, hop_l, in_r, in_l, y_out, y_in)]
    bufs_b = [r.at[1] for r in (hop_r, hop_l, in_r, in_l, y_out, y_in)]

    def slabs(chunk):
        return NEAR[:4] if chunk == 0 else NEAR[4:]

    def landed(full, sems, chunk):
        for k in slabs(chunk):
            net.arrive(full.at[(1 - net.c) * NZ + net.dz(k)], sems[k % NZ])

    def pairs(chunk):
        for i, k in enumerate(slabs(chunk)):
            for side in range(2):
                yield (chunk * 8 + i * 2 + side) * PAIR, side * NZ + net.dz(k)

    def pick_tok(chunk):
        for near, p in pairs(chunk):
            block = tok_all[p].reshape(2 * TOK, tok_all.shape[-1])
            at = pl.ds(pl.multiple_of(p * PAIR, 16), PAIR)
            sel = picker(rank_old, p).astype(BF)
            rows[pl.ds(near, PAIR), :] = jnp.dot(sel, block, preferred_element_type=F32).astype(BF)
            sel = picker(rank_new, p).astype(BF)
            rows_new[at, :] = jnp.dot(sel, block, preferred_element_type=F32).astype(BF)

    def pick_cot(chunk):
        for near, p in pairs(chunk):
            block = cot_all[p].reshape(2 * TOK, cot_all.shape[-1])
            at = pl.ds(pl.multiple_of(p * PAIR, 16), PAIR)
            for rank_ref, weight_ref, out, where in (
                (rank_old, weight_old, rows_b, pl.ds(near, PAIR)),
                (rank_new, weight_new, cot_new, at),
            ):
                hit = picker(rank_ref, p)
                weight = jnp.sum(hit * weight_ref[pl.ds(p, 1), :], axis=1, keepdims=True)
                sel = jnp.dot(hit.astype(BF), block, preferred_element_type=F32)
                out[where, :] = (sel * weight).astype(BF)

    def project(source, w, part, shift, chunk):
        where = cols(net.dx(shift))
        tile = 320

        def body(i, carry):
            at = pl.ds(pl.multiple_of(chunk * CHUNK + i * tile, tile), tile)
            part[at, where] = lax.dot_general(
                source[at, :], w[where, :], (((1,), (1,)), ((), ())), preferred_element_type=F32
            ).astype(BF)
            return carry

        lax.fori_loop(0, CHUNK // tile, body, 0)

    def flow(full, sems, pick, source, w, part, out, bufs, load, keep, chunk):
        landed(full, sems, chunk)
        pick(chunk)
        if chunk == 0:
            load.wait()
        else:
            keep.start()
        project(source, w, part, 2, chunk)
        red = reduce_flow(net, part, out, *bufs, chunk * CHUNK)
        next(red)
        project(source, w, part, 1, chunk)
        project(source, w, part, -1, chunk)
        next(red)
        project(source, w, part, 0, chunk)
        yield
        yield from red

    def spread_rows(out, value):
        for chunk in range(2):
            for near, p in pairs(chunk):
                out[pl.ds(pl.multiple_of(p * PAIR, 16), PAIR), :] = value(pl.ds(near, PAIR)).astype(BF)

    def act_hidden(at):
        pre = acc_a[at, :]
        return pre * jax.nn.sigmoid(pre)

    def act_slope(at):
        pre, back = acc_a[at, :], acc_b[at, :]
        sig = jax.nn.sigmoid(pre)
        return back * sig * (1.0 + pre * (1.0 - sig))

    flows = {
        "i": small_gather(net, info, info_all, local_sem.at[0]),
        "t": gather_flow(net, tok, tok_all, local_sem.at[1], tok_sems),
        "k": gather_flow(net, cot, cot_all, local_sem.at[2], cot_sems),
        "w": whole_flow(net, hid_s, hidden, local_sem.at[1]),
        "m": move_flow(net, hid_s, old, new, spread, picked, hid_moved, local_sem.at[2]),
    }
    for name, chunk in (("p", 0), ("q", 1)):
        flows[name] = flow(tok_all, tok_sems, pick_tok, rows, wg, part_a, acc_a, bufs_a, load_g, keep_rows, chunk)
    for name, chunk in (("u", 0), ("v", 1)):
        flows[name] = flow(cot_all, cot_sems, pick_cot, rows_b, wd, part_b, acc_b, bufs_b, load_d, keep_cot, chunk)
    me = net.z * 4 + net.h * 2 + net.c
    for step in FIRST:
        if step == "r":
            ranks(info_all, look_up(old, me, jnp.int32), rank_old, weight_old)
            ranks(info_all, look_up(new, me, jnp.int32), rank_new, weight_new)
        elif step == "h":
            spread_rows(hid_s, act_hidden)
        else:
            next(flows[step], None)
    keep_hidden.start()
    spread_rows(slope_o, act_slope)
    keep_rows.wait()
    keep_cot.wait()
    keep_hidden.wait()
    net.drain()


def dispatch(*args):
    width = args[0].shape[1]
    vm = pl.BlockSpec(memory_space=pltpu.VMEM)
    sm = pl.BlockSpec(memory_space=pltpu.SMEM)
    hbm = pl.BlockSpec(memory_space=pl.ANY)
    sds = jax.ShapeDtypeStruct
    half = ROWS // 2
    return pl.pallas_call(
        dispatch_kernel,
        out_shape=(
            sds((ROWS, 128), BF),
            sds((ROWS, 1024), BF),
            sds((ROWS, 128), BF),
            sds((ROWS, width), BF),
            sds((ROWS, width), BF),
            sds((16, 256), F32),
            sds((16, 256), F32),
        ),
        in_specs=[vm] * 3 + [hbm] * 2 + [sm] * 2,
        out_specs=(vm, hbm, vm, hbm, hbm, vm, vm),
        scratch_shapes=[
            pltpu.VMEM((1024, width), BF),
            pltpu.VMEM((1024, width), BF),
            pltpu.VMEM((ROWS, 1024), BF),
            pltpu.VMEM((ROWS, width), BF),
            pltpu.VMEM((ROWS, width), BF),
            pltpu.VMEM((16, 2, TOK, width), BF),
            pltpu.VMEM((16, 2, TOK, width), BF),
            pltpu.VMEM((2, 16, 16, 128), F32),
            pltpu.VMEM((ROWS, width), BF),
            pltpu.VMEM((ROWS, width), BF),
            pltpu.VMEM((ROWS, 1024), BF),
            pltpu.VMEM((ROWS, 1024), BF),
            pltpu.VMEM((ROWS, 128), F32),
            pltpu.VMEM((ROWS, 128), F32),
            pltpu.VMEM((2, half, 256), BF),
            pltpu.VMEM((2, half, 256), BF),
            pltpu.VMEM((2, ROWS, 256), BF),
            pltpu.VMEM((2, ROWS, 256), BF),
            pltpu.VMEM((2, ROWS, 128), BF),
            pltpu.VMEM((2, ROWS, 128), BF),
            pltpu.VMEM((16, 256), F32),
            pltpu.VMEM((16, 256), F32),
            pltpu.VMEM((ROWS, 128), BF),
            pltpu.VMEM((NZ, 4, ROWS // NZ, 128), BF),
            pltpu.VMEM((NZ, ROWS // NZ, 128), BF),
            pltpu.SemaphoreType.DMA((8,)),
            pltpu.SemaphoreType.DMA((256,)),
            pltpu.SemaphoreType.DMA((256,)),
        ],
        compiler_params=pltpu.CompilerParams(
            collective_id=0, has_side_effects=True, vmem_limit_bytes=VMEM_LIMIT
        ),
    )(*args)


def add_into(dst, *srcs):
    lead, rows = dst.shape[:-2], dst.shape[-2]

    def body(i, carry):
        at = pl.ds(pl.multiple_of(i * 16, 16), 16)
        for j in range(lead[0] if lead else 1):
            where = (j, at) if lead else (at,)
            acc = dst[where].astype(F32)
            for src in srcs:
                acc = acc + src[where].astype(F32)
            dst[where] = acc.astype(BF)
        return carry

    lax.fori_loop(0, rows // 16, body, 0)


def return_flow(net, contribution, to_core, from_core, sums, y_b, ring_ra, ring_la, ring_rb, ring_lb, y_a, out):
    z, h, c = net.z, net.h, net.c
    width = out.shape[-1]
    other_y, other_c = net.at(h=1 - h), net.at(c=1 - c)
    right, left = net.at(z=net.dz(1)), net.at(z=net.dz(-1))
    ra, rb = pl.ds(0, HALF), pl.ds(HALF, HALF)
    a_first, a_last = pl.ds(0, QUART), pl.ds(QUART, QUART)
    b_first, b_last = pl.ds(HALF, QUART), pl.ds(HALF + QUART, QUART)
    both = slice(None)
    core, yb = {}, {}

    def give(s):
        for k in ((4,), (3, -3), (2, -2), (1, -1), (0,), ())[s]:
            zt = net.dz(k)
            to_core[zt] = contribution((1 - c) * NZ + zt).astype(BF).reshape(2, TOK, width)
            core[k] = net.send(to_core.at[zt], from_core.at[zt], other_c)

    give(0)
    yield
    ar = al = br = bl = None
    for s in range(5):
        ks = (4,) if s == 0 else (0,) if s == 4 else (4 - s, s - 4)
        give(s + 1)
        for k in ks:
            zt = net.dz(k)
            net.arrive(from_core.at[zt], core[k])
            got = from_core[zt].astype(F32).reshape(2 * TOK, width)
            sums[zt] = (contribution(c * NZ + zt) + got).astype(BF).reshape(2, TOK, width)
            yb[k] = net.send(sums.at[zt, 1 - h, rb], y_b.at[zt], other_y)
        zr, zl = net.dz(4 - s), net.dz(s - 4)
        if s == 0:
            ar = net.send(sums.at[zr, both, a_first], ring_ra.at[0, both, a_first], right)
            al = net.send(sums.at[zr, both, a_last], ring_la.at[0, both, a_last], left)
            net.arrive(y_b.at[zr], yb[4])
            add_into(sums.at[zr, h, rb], y_b.at[zr])
            br = net.send(sums.at[zr, h, b_first], ring_rb.at[0, a_first], right)
            bl = net.send(sums.at[zr, h, b_last], ring_lb.at[0, a_last], left)
            yield
            continue
        at_r, at_l = (a_first, a_last) if s == 1 else (ra, ra)
        bt_r, bt_l = (b_first, b_last) if s == 1 else (rb, rb)
        if s < 4:
            net.arrive(ring_ra.at[s - 1, both, at_r], ar)
            add_into(sums.at[zr, both, at_r], ring_ra.at[s - 1, both, at_r])
            ar = net.send(sums.at[zr, both, ra], ring_ra.at[s], right)
            net.arrive(ring_la.at[s - 1, both, at_l], al)
            add_into(sums.at[zl, both, at_l], ring_la.at[s - 1, both, at_l])
            al = net.send(sums.at[zl, both, ra], ring_la.at[s], left)
            for k in ks:
                net.arrive(y_b.at[net.dz(k)], yb[k])
                add_into(sums.at[net.dz(k), h, rb], y_b.at[net.dz(k)])
            net.arrive(ring_rb.at[s - 1, at_r], br)
            add_into(sums.at[zr, h, bt_r], ring_rb.at[s - 1, at_r])
            br = net.send(sums.at[zr, h, rb], ring_rb.at[s], right)
            net.arrive(ring_lb.at[s - 1, at_l], bl)
            add_into(sums.at[zl, h, bt_l], ring_lb.at[s - 1, at_l])
            bl = net.send(sums.at[zl, h, rb], ring_lb.at[s], left)
            yield
            continue
        net.arrive(ring_ra.at[3], ar)
        net.arrive(ring_la.at[3], al)
        add_into(sums.at[z, both, ra], ring_ra.at[3], ring_la.at[3])
        ya = net.send(sums.at[z, 1 - h, ra], y_a, other_y)
        net.arrive(y_b.at[z], yb[0])
        net.arrive(ring_rb.at[3], br)
        net.arrive(ring_lb.at[3], bl)
        out[rb, :] = (
            sums[z, h, rb, :].astype(F32)
            + y_b[z].astype(F32)
            + ring_rb[3].astype(F32)
            + ring_lb[3].astype(F32)
        ).astype(BF)
        yield
        net.arrive(y_a, ya)
        out[ra, :] = (sums[z, h, ra, :].astype(F32) + y_a[...].astype(F32)).astype(BF)
    yield


ORDER = "bmf" "bf" "bf" "mhbf" "hbf" "mhbf" "mhsbf" "hsbd" "sb" "sb" "sb" "bg"


def finish_kernel(
    slope_s, hidden, hid_moved, rows_in, cot_in, rank, weight, wg_in, wd_in, old, new,
    layer_out, token_grads, grad_gate, grad_down,
    rows_new, cot_new, wg, wd,
    slope, hidden_new, slope_new, spread, picked, moved, out_rows, back_rows,
    to_core, from_core, sums, y_b, ring_ra, ring_la, ring_rb, ring_lb, y_a,
    local_sem, send_sem, recv_sem,
):
    net = Links(send_sem, recv_sem)
    loads = [
        pltpu.make_async_copy(src, dst, local_sem.at[4 + i])
        for i, (src, dst) in enumerate(((wd_in, wd), (wg_in, wg), (cot_in, cot_new), (rows_in, rows_new)))
    ]
    for load in loads:
        load.start()
    net.barrier()
    tile = 320

    def weighted(i, carry):
        at = pl.ds(pl.multiple_of(i * tile, tile), tile)
        w = jnp.concatenate(
            [
                jnp.sum(
                    picker(rank, i * 4 + j) * weight[pl.ds(i * 4 + j, 1), :], axis=1, keepdims=True
                )
                for j in range(4)
            ],
            axis=0,
        )
        out = jnp.dot(hidden[at, :], wd[...], preferred_element_type=F32)
        out_rows[at, :] = (out * w).astype(BF)
        return carry

    def plain(i, carry):
        at = pl.ds(pl.multiple_of(i * tile, tile), tile)
        back_rows[at, :] = jnp.dot(slope[at, :], wg[...], preferred_element_type=F32).astype(BF)
        return carry

    def placed(rows):
        def contribution(p):
            sel = picker(rank, p).astype(BF)
            at = pl.ds(pl.multiple_of(p * PAIR, 16), PAIR)
            return lax.dot_general(sel, rows[at, :], (((0,), (0,)), ((), ())), preferred_element_type=F32)

        return contribution

    def outer(left, right, out):
        def body(i, carry):
            at = pl.ds(pl.multiple_of(i * 256, 256), 256)
            out[at, :] = lax.dot_general(
                left[:, at], right[...], (((0,), (0,)), ((), ())), preferred_element_type=F32
            ).astype(BF)
            return carry

        lax.fori_loop(0, 4, body, 0)

    bufs = (to_core, from_core, sums, y_b, ring_ra, ring_la, ring_rb, ring_lb, y_a)

    def forward():
        loads[0].wait()
        lax.fori_loop(0, ROWS // tile, weighted, 0)
        yield from return_flow(net, placed(out_rows), *[b.at[0] for b in bufs], layer_out)

    def backward():
        yield from whole_flow(net, slope_s, slope, local_sem.at[0])
        loads[1].wait()
        lax.fori_loop(0, ROWS // tile, plain, 0)
        yield from return_flow(net, placed(back_rows), *[b.at[1] for b in bufs], token_grads)

    flows = {
        "b": backward(),
        "f": forward(),
        "m": move_flow(net, slope_s, old, new, spread, picked, moved, local_sem.at[1]),
        "h": whole_flow(net, hid_moved, hidden_new, local_sem.at[2]),
        "s": whole_flow(net, moved, slope_new, local_sem.at[3]),
    }
    for step in ORDER:
        if step == "d":
            loads[2].wait()
            outer(hidden_new, cot_new, grad_down)
        elif step == "g":
            loads[3].wait()
            outer(slope_new, rows_new, grad_gate)
        else:
            next(flows[step], None)
    net.drain()


def finish(*args):
    width = args[3].shape[1]
    vm = pl.BlockSpec(memory_space=pltpu.VMEM)
    sm = pl.BlockSpec(memory_space=pltpu.SMEM)
    hbm = pl.BlockSpec(memory_space=pl.ANY)
    sds = jax.ShapeDtypeStruct
    n = ROWS // NZ
    return pl.pallas_call(
        finish_kernel,
        out_shape=(
            sds((TOK, width), BF),
            sds((TOK, width), BF),
            sds((1024, width), BF),
            sds((1024, width), BF),
        ),
        in_specs=[vm] * 3 + [hbm] * 2 + [vm] * 2 + [hbm] * 2 + [sm] * 2,
        out_specs=(vm,) * 4,
        scratch_shapes=[
            pltpu.VMEM((ROWS, width), BF),
            pltpu.VMEM((ROWS, width), BF),
            pltpu.VMEM((1024, width), BF),
            pltpu.VMEM((1024, width), BF),
            pltpu.VMEM((ROWS, 1024), BF),
            pltpu.VMEM((ROWS, 1024), BF),
            pltpu.VMEM((ROWS, 1024), BF),
            pltpu.VMEM((NZ, 4, n, 128), BF),
            pltpu.VMEM((NZ, n, 128), BF),
            pltpu.VMEM((ROWS, 128), BF),
            pltpu.VMEM((ROWS, width), BF),
            pltpu.VMEM((ROWS, width), BF),
            pltpu.VMEM((2, NZ, 2, TOK, width), BF),
            pltpu.VMEM((2, NZ, 2, TOK, width), BF),
            pltpu.VMEM((2, NZ, 2, TOK, width), BF),
            pltpu.VMEM((2, NZ, HALF, width), BF),
            pltpu.VMEM((2, 4, 2, HALF, width), BF),
            pltpu.VMEM((2, 4, 2, HALF, width), BF),
            pltpu.VMEM((2, 4, HALF, width), BF),
            pltpu.VMEM((2, 4, HALF, width), BF),
            pltpu.VMEM((2, HALF, width), BF),
            pltpu.SemaphoreType.DMA((8,)),
            pltpu.SemaphoreType.DMA((256,)),
            pltpu.SemaphoreType.DMA((256,)),
        ],
        compiler_params=pltpu.CompilerParams(
            collective_id=1, has_side_effects=True, vmem_limit_bytes=VMEM_LIMIT
        ),
    )(*args)


def hand_out_kernel(a, b, c, d, a_o, b_o, c_o, d_o, a_v, b_v, c_v, d_v, load_sem, store_sem):
    loads, stores = [], []
    for src, mid, dst, parts in ((c, c_v, c_o, 4), (d, d_v, d_o, 4), (a, a_v, a_o, 1), (b, b_v, b_o, 1)):
        n = src.shape[0] // parts
        for i in range(parts):
            rows = pl.ds(i * n, n)
            k = len(loads)
            loads.append(pltpu.make_async_copy(src.at[rows], mid.at[rows], load_sem.at[k]))
            stores.append(pltpu.make_async_copy(mid.at[rows], dst.at[rows], store_sem.at[k]))
    for load in loads:
        load.start()
    for load, store in zip(loads, stores):
        load.wait()
        store.start()
    for store in stores:
        store.wait()


def hand_out(*results):
    hbm = pl.BlockSpec(memory_space=pl.ANY)
    return pl.pallas_call(
        hand_out_kernel,
        out_shape=tuple(jax.ShapeDtypeStruct(r.shape, r.dtype) for r in results),
        in_specs=[hbm] * 4,
        out_specs=(hbm,) * 4,
        scratch_shapes=[pltpu.VMEM(r.shape, r.dtype) for r in results]
        + [pltpu.SemaphoreType.DMA((10,)), pltpu.SemaphoreType.DMA((10,))],
        compiler_params=pltpu.CompilerParams(vmem_limit_bytes=VMEM_LIMIT),
    )(*results)


def per_device(tokens, cotangent, expert_ids, gate_weights, owner_old, owner_new, w_gate, w_down):
    info = jnp.concatenate([expert_ids.T.astype(F32), gate_weights.T], axis=0)
    gate_here, down_here = w_gate[0], w_down[0]
    slope_s, hidden, hid_moved, rows_new, cot_new, rank, weight = dispatch(
        tokens, cotangent, info, gate_here, down_here, owner_old, owner_new
    )
    results = finish(
        slope_s, hidden, hid_moved, rows_new, cot_new, rank, weight, gate_here, down_here, owner_old, owner_new
    )
    layer_out, token_grads, grad_gate, grad_down = hand_out(*results)
    return (layer_out, token_grads, grad_gate[None], grad_down[None])


def solution(mesh):
    return jax.shard_map(
        per_device,
        mesh=mesh,
        in_specs=(
            P("expert", "hid"),
            P("expert", "hid"),
            P("expert", None),
            P("expert", None),
            P(),
            P(),
            P("expert", None, "hid"),
            P("expert", None, "hid"),
        ),
        out_specs=(
            P("expert", "hid"),
            P("expert", "hid"),
            P("expert", None, "hid"),
            P("expert", None, "hid"),
        ),
        check_vma=False,
    )
```
